512 devices in a mesh: grp: 16 (over z, core), vox: 32 (over x, y).
Axes of the slice: x: 4, y: 8, z: 8, core: 2. Of those that a mesh axis runs over, the one named last changes fastest.
Arguments:
- log_modulus: float32 [384, 262144], P('grp', 'vox'), may hold values from -3 to 3
- basis: bfloat16 [1024, 128], replicated, may hold values from -0.1875 to 0.1875
- sensitivity: bfloat16 [32768, 128], P('vox'), may hold values from -0.5 to 0.5
- obs_block: int32 [32768, 1], P('vox'), may hold values from 0 to 255; in each aligned block of 1024 rows (0 to 1023, 1024 to 2047, ...) at most 8 rows name the same one
- observed: float32 [32768], P('vox'), may hold values from -9 to 9
- noise_scale: float32 [32768], P('vox'), may hold values from 0.5 to 2
- perturbation: float32 [384, 32768], P('grp', 'vox'), may hold values from -6 to 6
Outputs:
- updated: float32 [384, 262144], P('grp', 'vox')
The draws below stay inside these ranges and needn't reach their ends.
Inputs may be any that keep to these rules, and one draw needn't show every extreme that they name: `obs_block`: among the observations of one index of vox (aligned blocks of 1024 rows), no voxel block is read by more than 8 of them, and in every draw some block is read by exactly 8.
All inputs are finite; a program needn't handle non-finite values.
Results may differ from the reference program's by a relative error of at most 0.011.
Values may be sent and summed in bfloat16 or wider, within the bound.
A program may use at most 64 MiB of HBM per device.

```python
import math
import jax
import jax.numpy as jnp
import numpy as np
from jax import lax

J_DEV = 24
OBS_DEV = 1024
BV = 1024
F = 128
J = 384
NB = 256
NV = 262144
NO = 32768
CAPB = 8
N_GRP = 16


def steps_of(rng, dims, split, least, largest):
    loudness = 1.0
    for dim, shards_of in split:
        draws = jax.random.uniform(jax.random.fold_in(jax.random.fold_in(rng, 6), dim), (shards_of,), jnp.float32, least / len(split), largest / len(split))
        loudness = loudness * jnp.repeat(jnp.exp(draws), dims[dim] // shards_of).reshape((-1,) + (1,) * (len(dims) - 1 - dim))
    return loudness


def deal_out(own_key, own, number, rows, number_of, top, reach, lean):
    sequence = jax.random.permutation(own_key, number_of)
    packed, ordinary = load_shares(number_of, rows * top, reach, lean, True), load_shares(number_of, rows * top, reach, lean, False)
    places = jnp.arange(number_of)

    def named(lengths, offset_by):
        used = int((lengths > 0).sum())
        fixed = max(1, used // 4)
        shifted = fixed + (places - fixed + offset_by * (used - fixed)) % max(1, number_of - fixed)
        return jnp.zeros((number_of,), jnp.int32).at[sequence[jnp.where(places < fixed, places, shifted)]].set(jnp.asarray(lengths, jnp.int32))

    lengths = jnp.where(number % 4 == 0, named(packed, number // 4), named(ordinary, number - number // 4 - 1))
    mixed = jax.random.permutation(jax.random.fold_in(own, 3), number_of)
    giver, sink = mixed[0:number_of // 2 * 2:2], mixed[1:number_of // 2 * 2:2]
    room = jnp.minimum(lengths[giver] - 1, reach - lengths[sink]) // 2
    room = jnp.where((giver == sequence[0]) | (sink == sequence[0]) | (lengths[sink] == 0), 0, jnp.maximum(room, 0))
    shifted = jax.random.randint(jax.random.fold_in(own, 4), (number_of // 2,), 0, 1 << 20) % (room + 1)
    lengths = lengths.at[giver].add(-shifted).at[sink].add(shifted)
    items = jnp.searchsorted(jnp.cumsum(lengths), jnp.arange(rows * top), side="right").astype(jnp.int32)
    grid = items.reshape(top, rows).T
    grid = grid[jax.random.permutation(jax.random.fold_in(own, 1), rows)]
    offset_by = jax.random.randint(jax.random.fold_in(own, 2), (rows, 1), 0, top)
    return jnp.take_along_axis(grid, (jnp.arange(top)[None, :] + offset_by) % top, axis=1)


def load_shares(amount, total, reach, slope, full):
    weights = [(1 << 20) // math.isqrt(rank ** slope) + 1 for rank in range(1, amount + 1)]
    largest = reach if full else min(reach, max(-(-total // amount), total * weights[0] // sum(weights)))
    least = 1 if total - largest >= amount - 1 else 0
    counts, rest = [largest] + [least] * (amount - 1), total - largest - least * (amount - 1)
    while rest > 0:
        free = [i for i in range(1, amount) if counts[i] < largest] or [i for i in range(1, amount) if counts[i] < reach]
        mass, left = sum([weights[i] for i in free]), rest
        for i in free:
            more = min(reach - counts[i], max(1, left * weights[i] // mass), rest)
            counts[i] = counts[i] + more
            rest = rest - more
    return np.array(counts)


def centred(rng, dims, width, limit, pieces=(), kind=jnp.bfloat16):
    result = width * jax.random.normal(rng, dims, jnp.float32)
    if pieces:
        result = result * steps_of(rng, dims, pieces, -0.22, 0.18)
    return jnp.clip(result, -limit, limit).astype(kind)


def setup_inputs(seed: int = 0) -> dict:
    splits = jax.random.split(jax.random.key(seed), 8)
    log_modulus = centred(splits[0], (J, NV), 0.5, 3.0, ((0, 16), (1, 32)), jnp.float32)
    basis = centred(splits[1], (BV, F), BV ** -0.5, 0.1875)
    sensitivity = centred(splits[2], (NO, F), F ** -0.5, 0.5, ((0, 32),))
    obs_block_keys = jax.random.split(jax.random.fold_in(splits[3], 1), NO // OBS_DEV)
    obs_block_turns = jax.random.permutation(jax.random.fold_in(splits[3], 3), NO // OBS_DEV)
    obs_block = jax.vmap(lambda own, number: deal_out(jax.random.fold_in(splits[3], 2), own, number, OBS_DEV, NB, 1, CAPB, 1))(obs_block_keys, obs_block_turns).reshape((NO, 1))
    observed = centred(splits[4], (NO,), 1.5, 9.0, ((0, 32),), jnp.float32)
    noise_scale = jnp.clip(jnp.exp(math.log(2.0) - 1.3862944 * jax.random.uniform(splits[5], (NO,), jnp.float32) ** steps_of(splits[5], (NO,), ((0, 32),), -0.2, 0.2)), 0.5, 2.0)
    perturbation = centred(splits[6], (J, NO), 1.0, 6.0, ((0, 16), (1, 32)), jnp.float32)
    return {"log_modulus": log_modulus, "basis": basis, "sensitivity": sensitivity, "obs_block": obs_block, "observed": observed, "noise_scale": noise_scale, "perturbation": perturbation}


def reference(log_modulus, basis, sensitivity, obs_block, observed, noise_scale, perturbation):
    members = J_DEV * N_GRP
    compliance = jnp.exp(-log_modulus).astype(jnp.bfloat16)
    features = jnp.dot(compliance.reshape(members * NB, BV).astype(jnp.float32), basis.astype(jnp.float32), preferred_element_type=jnp.float32)
    features = features.astype(jnp.bfloat16).reshape(members, NB, F)
    blocks = obs_block[:, 0].astype(jnp.int32)
    sens_wide = sensitivity.astype(jnp.float32)

    def predict(member_feat):
        return lax.optimization_barrier(jnp.sum(sens_wide * member_feat[blocks].astype(jnp.float32), axis=1))
    predicted = lax.map(predict, features)
    scale_root = math.sqrt(members - 1)
    centre = lax.optimization_barrier(jnp.mean(predicted, axis=0))
    scaled = ((predicted - centre) / (noise_scale * scale_root)).astype(jnp.bfloat16)
    misfit = ((observed - predicted) / noise_scale + perturbation).astype(jnp.bfloat16)
    misfit_wide = misfit.astype(jnp.float32)
    damping = jnp.sum(misfit_wide * misfit_wide) / (members * NO)
    contract = (((1,), (1,)), ((), ()))
    gram_total = lax.dot_general(scaled.astype(jnp.float32), scaled.astype(jnp.float32), contract, preferred_element_type=jnp.float32)
    cross_total = lax.dot_general(scaled.astype(jnp.float32), misfit.astype(jnp.float32), contract, preferred_element_type=jnp.float32)
    system = gram_total + damping * jnp.eye(members, dtype=jnp.float32)
    factor = jnp.linalg.cholesky(system)
    halfway = lax.linalg.triangular_solve(factor, cross_total, left_side=True, lower=True)
    weights = lax.linalg.triangular_solve(factor, halfway, left_side=True, lower=True, transpose_a=True)
    weights_low = weights.astype(jnp.bfloat16)
    anomaly = log_modulus.astype(jnp.bfloat16)
    mixture = lax.dot_general(weights_low.astype(jnp.float32), anomaly.astype(jnp.float32), (((0,), (0,)), ((), ())), preferred_element_type=jnp.float32)
    return log_modulus + mixture / scale_root
```

```python
import functools
import math

import jax
import jax.numpy as jnp
from jax import lax
from jax.experimental import pallas as pl
from jax.experimental.pallas import tpu as pltpu
from jax.sharding import PartitionSpec as P

MESH = pl.DeviceIdType.MESH
HIGHEST = lax.Precision.HIGHEST
NX, NY, NZ, NC = 4, 8, 8, 2
N_VOX, N_GRP = NX * NY, NZ * NC
SIDE = 128
PIVOTS = 4
TILE = (8, 128)


def remote(src, dst, send_sem, recv_sem, device):
    return pltpu.make_async_remote_copy(
        src_ref=src, dst_ref=dst, send_sem=send_sem, recv_sem=recv_sem,
        device_id=device, device_id_type=MESH,
    )


def exchange_kernel(
    lm_ref, basis_ref, sens_ref, blk_ref, obs_ref, noise_ref, pert_ref,
    gram_ref, cross_ref, damp_ref,
    fbuf, sens_t, pred, dbuf, mbuf, sbuf, part, rbuf, tot, gbuf,
    xs_sem, xr_sem, ys_sem, yr_sem,
    ds_sem, dr_sem, ms_sem, mr_sem, dps_sem, dpr_sem, mps_sem, mpr_sem,
    rs_sem, rr_sem, as_sem, ar_sem, gs_sem, gr_sem, gps_sem, gpr_sem,
):
    g = lax.axis_index("grp")
    v = lax.axis_index("vox")
    z, core = g // NC, g % NC
    x, y = v // NY, v % NY
    partner = z * NC + (1 - core)
    j_dev, vox_dev = lm_ref.shape
    block_vox, width = basis_ref.shape
    blocks_dev = vox_dev // block_vox
    n_obs = sens_ref.shape[0]
    half = n_obs // 2
    members = j_dev * N_GRP
    scale_root = math.sqrt(members - 1)

    barrier = pltpu.get_barrier_semaphore()

    def greet_vox(i, _):
        pl.semaphore_signal(barrier, inc=1, device_id={"vox": (v + i) % N_VOX}, device_id_type=MESH)
        return 0

    def z_peer(i):
        return ((z + i) % NZ) * NC + core

    def greet_grp(i, _):
        pl.semaphore_signal(barrier, inc=1, device_id={"grp": z_peer(i)}, device_id_type=MESH)
        return 0

    lax.fori_loop(1, N_VOX, greet_vox, 0)
    lax.fori_loop(1, NZ, greet_grp, 0)
    pl.semaphore_signal(barrier, inc=1, device_id={"grp": partner}, device_id_type=MESH)

    lm = lm_ref[...]
    compliance = jnp.exp(-lm)
    stacked = jnp.concatenate(
        [compliance[:, b * block_vox : (b + 1) * block_vox] for b in range(blocks_dev)], axis=0
    ).astype(jnp.bfloat16)
    features = jnp.dot(stacked, basis_ref[...], preferred_element_type=jnp.float32)
    fbuf[y, x] = features.astype(jnp.bfloat16)
    pl.semaphore_wait(barrier, N_VOX - 1 + NZ - 1 + 1)

    def x_copy(i):
        src = (x + NX - i) % NX
        mine = remote(fbuf.at[y, x], fbuf.at[y, x], xs_sem.at[i], xr_sem.at[i],
                      {"vox": ((x + i) % NX) * NY + y})
        theirs = remote(fbuf.at[y, src], fbuf.at[y, src], xs_sem.at[i], xr_sem.at[i],
                        {"vox": ((x + i) % NX) * NY + y})
        return mine, theirs

    def y_copy(way, step, xi, arriving):
        turn = 1 if way == 0 else NY - 1
        xs = (x + xi) % NX
        back = step if arriving else step - 1
        ys = (y + (NY - turn) * back) % NY
        slot = fbuf.at[ys, xs]
        return remote(slot, slot, ys_sem.at[way, step - 1, xi], yr_sem.at[way, step - 1, xi],
                      {"vox": x * NY + (y + turn) % NY}), ys, xs

    def y_send(way, step, xi):
        y_copy(way, step, xi, False)[0].start()

    for i in (1, NX - 1, 2):
        x_copy(i)[0].start()
    y_send(0, 1, 0)
    y_send(1, 1, 0)
    sens_t[...] = sens_ref[...].T
    pred[...] = jnp.zeros_like(pred)
    blk = blk_ref[...]

    def compute(ys, xs):
        all_pred = jnp.dot(fbuf[ys, xs], sens_t[...], preferred_element_type=jnp.float32)
        first = (xs * NY + ys) * blocks_dev
        acc = pred[...]
        for b in range(blocks_dev):
            acc = jnp.where(blk == first + b, all_pred[b * j_dev : (b + 1) * j_dev], acc)
        pred[...] = acc

    compute(y, x)

    def far(n):
        return n + n // 2 - 2 * (n // 3)

    def x_turn(n, _):
        xi = far(n)
        i = NX - xi
        x_copy(i)[1].wait_recv()
        y_send(0, 1, xi)
        y_send(1, 1, xi)
        compute(y, (x + xi) % NX)
        return 0

    lax.fori_loop(1, NX, x_turn, 0)
    last = NY // 2

    def y_turn(n, _):
        step, xi = n // NX + 1, far(n % NX)
        low = n % NX < NX // 2
        up, up_y, xs = y_copy(0, step, xi, True)
        up.wait_recv()

        @pl.when((step + 1 < last) | low)
        def _():
            y_send(0, step + 1, xi)

        down, down_y, _ = y_copy(1, step, xi, True)
        down.wait_recv()

        @pl.when((step + 1 < last) | jnp.logical_not(low))
        def _():
            y_send(1, step + 1, xi)

        compute(up_y, xs)
        compute(down_y, xs)
        return 0

    lax.fori_loop(0, (last - 1) * NX, y_turn, 0)

    def y_last(n, _):
        xi = far(n)

        @pl.when(n < NX // 2)
        def _():
            y_copy(0, last, xi, True)[0].wait_recv()

        @pl.when(n >= NX // 2)
        def _():
            y_copy(1, last, xi, True)[0].wait_recv()

        compute((y + last) % NY, (x + xi) % NX)
        return 0

    lax.fori_loop(0, NX, y_last, 0)

    own_pred = pred[...]
    own_mean = jnp.mean(own_pred, axis=0, keepdims=True)
    mbuf[g] = own_mean
    dev = own_pred - own_mean
    dbuf[g] = jnp.concatenate([dev[:, :half], dev[:, half:]], axis=0).astype(jnp.bfloat16)

    def peer_copies(i, arriving):
        slot = ((z + NZ - i) % NZ) * NC + core if arriving else g
        to = {"grp": z_peer(i)}
        return (remote(dbuf.at[slot], dbuf.at[slot], ds_sem.at[i], dr_sem.at[i], to),
                remote(mbuf.at[slot], mbuf.at[slot], ms_sem.at[i], mr_sem.at[i], to))

    def partner_copies(i, arriving):
        slot = ((z + NZ - i) % NZ) * NC + (1 - core if arriving else core)
        to = {"grp": partner}
        return (remote(dbuf.at[slot], dbuf.at[slot], dps_sem.at[i], dpr_sem.at[i], to),
                remote(mbuf.at[slot], mbuf.at[slot], mps_sem.at[i], mpr_sem.at[i], to))

    def send_peer(i, _):
        for copy in peer_copies(i, False):
            copy.start()
        return 0

    def forward(i, _):
        for copy in peer_copies(i, True):
            copy.wait_recv()
        for copy in partner_copies(i, False):
            copy.start()
        return 0

    def from_partner(i, _):
        for copy in partner_copies(i, True):
            copy.wait_recv()
        return 0

    lax.fori_loop(1, NZ, send_peer, 0)
    for copy in partner_copies(0, False):
        copy.start()
    noise = noise_ref[...]
    scale = 1.0 / (noise * scale_root)
    misfit = ((obs_ref[...] - own_pred) / noise + pert_ref[...]).astype(jnp.bfloat16)
    misfit_wide = misfit.astype(jnp.float32)
    squares = misfit_wide * misfit_wide
    lax.fori_loop(1, NZ, forward, 0)
    lax.fori_loop(0, NZ, from_partner, 0)

    centre = jnp.sum(mbuf[...], axis=0) * (1.0 / N_GRP)

    def scaled_of(group):
        d = dbuf[group].astype(jnp.float32)
        wide = jnp.concatenate([d[:j_dev], d[j_dev:]], axis=1)
        return (wide + (mbuf[group] - centre)) * scale

    def scale_pair(n, _):
        both = jnp.concatenate([scaled_of(2 * n), scaled_of(2 * n + 1)], axis=0)
        rows = 2 * j_dev
        sbuf[pl.ds(pl.multiple_of(n * rows, 16), rows), :] = both.astype(jnp.bfloat16)
        return 0

    lax.fori_loop(0, NZ, scale_pair, 0)
    left = jnp.concatenate([scaled_of(g), misfit_wide], axis=0).astype(jnp.bfloat16)
    sums = lax.dot_general(left, sbuf[...], (((1,), (1,)), ((), ())), preferred_element_type=jnp.float32)

    n_row, n_col = j_dev // 8, members // 128
    n_gram = n_row * n_col
    n_tiles = 2 * n_gram + 1
    for h in range(2):
        for i in range(n_row):
            for c in range(n_col):
                t = h * (n_gram + 1) + i * n_col + c
                part[t] = sums[h * j_dev + 8 * i : h * j_dev + 8 * i + 8, 128 * c : 128 * c + 128]
    folded = squares[0:8]
    for i in range(1, n_row):
        folded = folded + squares[8 * i : 8 * i + 8]
    lanes = folded[:, 0:128]
    for c in range(1, n_obs // 128):
        lanes = lanes + folded[:, 128 * c : 128 * c + 128]
    part[n_gram] = lanes

    def send_part(i, _):
        t = (v + i) % n_tiles

        @pl.when(t != v)
        def _():
            remote(part.at[t], rbuf.at[v], rs_sem, rr_sem, {"vox": t}).start()

        return 0

    lax.fori_loop(0, n_tiles, send_part, 0)

    @pl.when(v < n_tiles)
    def _():
        rbuf[v] = part[v]
        got = rbuf.at[pl.ds(0, N_VOX - 1)]
        pltpu.make_async_copy(got, got, rr_sem).wait()
        tot[v] = jnp.sum(rbuf[...], axis=0)

        def spread(i, _):
            remote(tot.at[v], tot.at[v], as_sem, ar_sem, {"vox": (v + i) % N_VOX}).start()
            return 0

        lax.fori_loop(1, N_VOX, spread, 0)
        most = tot.at[pl.ds(0, n_tiles - 1)]
        pltpu.make_async_copy(most, most, ar_sem).wait()

    @pl.when(v >= n_tiles)
    def _():
        whole = tot.at[pl.ds(0, n_tiles)]
        pltpu.make_async_copy(whole, whole, ar_sem).wait()

    gbuf[g] = tot[0 : n_gram + 1]

    def rows_copy(i, arriving):
        slot = gbuf.at[((z + NZ - i) % NZ) * NC + core if arriving else g]
        return remote(slot, slot, gs_sem.at[i], gr_sem.at[i], {"grp": z_peer(i)})

    def rows_partner(i, arriving):
        slot = gbuf.at[((z + NZ - i) % NZ) * NC + (1 - core if arriving else core)]
        return remote(slot, slot, gps_sem.at[i], gpr_sem.at[i], {"grp": partner})

    def rows_send(i, _):
        rows_copy(i, False).start()
        return 0

    def rows_forward(i, _):
        rows_copy(i, True).wait_recv()
        rows_partner(i, False).start()
        return 0

    def rows_from(i, _):
        rows_partner(i, True).wait_recv()
        return 0

    lax.fori_loop(1, NZ, rows_send, 0)
    rows_partner(0, False).start()
    for i in range(n_row):
        for c in range(n_col):
            cross_ref[8 * i : 8 * i + 8, 128 * c : 128 * c + 128] = tot[n_gram + 1 + i * n_col + c]
    lax.fori_loop(1, NZ, rows_forward, 0)
    lax.fori_loop(0, NZ, rows_from, 0)

    def place(n, _):
        for i in range(n_row):
            row = pl.multiple_of(n * j_dev + 8 * i, 8)
            for c in range(n_col):
                gram_ref[pl.ds(row, 8), 128 * c : 128 * c + 128] = gbuf[n, i * n_col + c]
        return 0

    lax.fori_loop(0, N_GRP, place, 0)
    squares_all = jnp.sum(gbuf[:, n_gram], axis=0)
    damping = jnp.sum(squares_all, keepdims=True) * (1.0 / (members * n_obs * N_VOX))
    damp_ref[...] = jnp.broadcast_to(damping, TILE)

    for i in range(1, NX):
        x_copy(i)[0].wait_send()

    def y_sent(n, _):
        step, xi = n // NX + 1, far(n % NX)
        low = n % NX < NX // 2

        @pl.when((step < last) | low)
        def _():
            y_copy(0, step, xi, False)[0].wait_send()

        @pl.when((step < last) | jnp.logical_not(low))
        def _():
            y_copy(1, step, xi, False)[0].wait_send()

        return 0

    lax.fori_loop(0, last * NX, y_sent, 0)

    def grp_sent(i, _):
        for copy in (*peer_copies(i, False), rows_copy(i, False)):
            copy.wait_send()
        return 0

    def partner_sent(i, _):
        for copy in (*partner_copies(i, False), rows_partner(i, False)):
            copy.wait_send()
        return 0

    lax.fori_loop(1, NZ, grp_sent, 0)
    lax.fori_loop(0, NZ, partner_sent, 0)

    @pl.when(v < n_tiles)
    def _():
        sent = part.at[pl.ds(0, n_tiles - 1)]
        pltpu.make_async_copy(sent, sent, rs_sem).wait()
        spread_all = rbuf.at[pl.ds(0, N_VOX - 1)]
        pltpu.make_async_copy(spread_all, spread_all, as_sem).wait()

    @pl.when(v >= n_tiles)
    def _():
        sent = part.at[pl.ds(0, n_tiles)]
        pltpu.make_async_copy(sent, sent, rs_sem).wait()


def exchange(log_modulus, basis, sensitivity, blocks, observed, noise, perturbation):
    j_dev, vox_dev = log_modulus.shape
    block_vox, width = basis.shape
    blocks_dev = vox_dev // block_vox
    n_obs = sensitivity.shape[0]
    members = j_dev * N_GRP
    n_gram = (j_dev // 8) * (members // 128)
    n_tiles = 2 * n_gram + 1
    f32, bf16 = jnp.float32, jnp.bfloat16
    dma = pltpu.SemaphoreType.DMA
    vmem = pl.BlockSpec(memory_space=pltpu.VMEM)
    return pl.pallas_call(
        exchange_kernel,
        out_shape=(
            jax.ShapeDtypeStruct((members, members), f32),
            jax.ShapeDtypeStruct((j_dev, members), f32),
            jax.ShapeDtypeStruct(TILE, f32),
        ),
        in_specs=[vmem] * 7,
        out_specs=(vmem,) * 3,
        scratch_shapes=[
            pltpu.VMEM((NY, NX, blocks_dev * j_dev, width), bf16),
            pltpu.VMEM((width, n_obs), bf16),
            pltpu.VMEM((j_dev, n_obs), f32),
            pltpu.VMEM((N_GRP, 2 * j_dev, n_obs // 2), bf16),
            pltpu.VMEM((N_GRP, 1, n_obs), f32),
            pltpu.VMEM((members, n_obs), bf16),
            pltpu.VMEM((n_tiles, *TILE), f32),
            pltpu.VMEM((N_VOX, *TILE), f32),
            pltpu.VMEM((n_tiles, *TILE), f32),
            pltpu.VMEM((N_GRP, n_gram + 1, *TILE), f32),
            dma((NX,)), dma((NX,)), dma((2, NY // 2, NX)), dma((2, NY // 2, NX)),
            dma((NZ,)), dma((NZ,)), dma((NZ,)), dma((NZ,)),
            dma((NZ,)), dma((NZ,)), dma((NZ,)), dma((NZ,)),
            dma, dma, dma, dma,
            dma((NZ,)), dma((NZ,)), dma((NZ,)), dma((NZ,)),
        ],
        compiler_params=pltpu.CompilerParams(
            collective_id=0, has_side_effects=True, vmem_limit_bytes=40 << 20
        ),
        name="exchange",
    )(log_modulus, basis, sensitivity, blocks, observed, noise, perturbation)


def product(a, b):
    return lax.dot_general(
        a, b, (((1,), (0,)), ((), ())), precision=HIGHEST, preferred_element_type=jnp.float32
    )


def inverse(d, k):
    n = d.shape[0]
    lane = lax.broadcasted_iota(jnp.int32, (1, n), 1)
    sub = lax.broadcasted_iota(jnp.int32, (n, 1), 0)
    for p in range(0, n, k):
        cols = [jnp.broadcast_to(d[:, p + j : p + j + 1], (n, n)) for j in range(k)]
        s = [[cols[j][p + i : p + i + 1] for j in range(k)] for i in range(k)]
        inside = (lane >= p) & (lane < p + k)
        rows = [
            jnp.where(inside, (lane == p + i).astype(jnp.float32), d[p + i : p + i + 1])
            for i in range(k)
        ]
        for i in range(k):
            inv = 1.0 / s[i][i]
            rows[i] = rows[i] * inv
            for j in range(i + 1, k):
                s[i][j] = s[i][j] * inv
            for r in range(k):
                if r != i:
                    rows[r] = rows[r] - s[r][i] * rows[i]
                    for j in range(i + 1, k):
                        s[r][j] = s[r][j] - s[r][i] * s[i][j]
        row_in = (sub >= p) & (sub < p + k)
        d = jnp.where(inside | row_in, 0.0, d)
        for j in range(k):
            d = d - jnp.where(row_in, jnp.where(sub == p + j, -1.0, 0.0), cols[j]) * rows[j]
    return d


def solve_kernel(gram_ref, cross_ref, damp_ref, out_ref):
    b = SIDE
    damp = damp_ref[0:1, :]
    eye = lax.broadcasted_iota(jnp.int32, (b, b), 0) == lax.broadcasted_iota(jnp.int32, (b, b), 1)

    def block(i, j):
        found = gram_ref[i * b : (i + 1) * b, j * b : (j + 1) * b]
        return found + jnp.where(eye, damp, 0.0) if i == j else found

    c0, c1, c2 = (cross_ref[:, i * b : (i + 1) * b] for i in range(3))
    a01, a02, a12 = block(0, 1), block(0, 2), block(1, 2)
    a10, a20, a21 = block(1, 0), block(2, 0), block(2, 1)
    i0 = inverse(block(0, 0), PIVOTS)
    u01 = product(i0, a01)
    u02 = product(i0, a02)
    y0 = product(c0, i0)
    i1 = inverse(block(1, 1) - product(a10, u01), PIVOTS)
    a12 = a12 - product(a10, u02)
    a21 = a21 - product(a20, u01)
    a22 = block(2, 2) - product(a20, u02)
    z1 = c1 - product(y0, a01)
    z2 = c2 - product(y0, a02)
    u12 = product(i1, a12)
    y1 = product(z1, i1)
    i2 = inverse(a22 - product(a21, u12), PIVOTS)
    z2 = z2 - product(y1, a12)
    x2 = product(z2, i2)
    x1 = product(z1 - product(x2, a21), i1)
    x0 = product(c0 - product(x1, a10) - product(x2, a20), i0)
    out_ref[...] = jnp.concatenate([x0, x1, x2], axis=1)


def solve(gram, cross, damping):
    vmem = pl.BlockSpec(memory_space=pltpu.VMEM)
    return pl.pallas_call(
        solve_kernel,
        out_shape=jax.ShapeDtypeStruct(cross.shape, jnp.float32),
        in_specs=[vmem] * 3,
        out_specs=vmem,
        compiler_params=pltpu.CompilerParams(vmem_limit_bytes=32 << 20),
        name="solve",
    )(gram, cross, damping)


def on_device(log_modulus, basis, sensitivity, obs_block, observed, noise_scale, perturbation):
    n_obs = sensitivity.shape[0]
    members = log_modulus.shape[0] * N_GRP
    anomaly = lax.all_gather(log_modulus.astype(jnp.bfloat16), "grp", axis=0, tiled=True)
    gram, cross, damping = exchange(
        log_modulus, basis, sensitivity, obs_block.reshape(1, n_obs),
        observed.reshape(1, n_obs), noise_scale.reshape(1, n_obs), perturbation,
    )
    weights = solve(gram, cross, damping).astype(jnp.bfloat16)
    mixture = jnp.dot(weights, anomaly, preferred_element_type=jnp.float32)
    return log_modulus + mixture / math.sqrt(members - 1)


def solution(mesh):
    in_specs = (
        P("grp", "vox"), P(), P("vox", None), P("vox", None), P("vox"), P("vox"), P("grp", "vox"),
    )
    return jax.shard_map(
        on_device, mesh=mesh, in_specs=in_specs, out_specs=P("grp", "vox"), check_vma=False
    )
```

```python
import functools
import math

import jax
import jax.numpy as jnp
from jax import lax
from jax.experimental import pallas as pl
from jax.experimental.pallas import tpu as pltpu
from jax.sharding import PartitionSpec as P

MESH = pl.DeviceIdType.MESH
HIGHEST = lax.Precision.HIGHEST
NX, NY, NZ, NC = 4, 8, 8, 2
N_VOX, N_GRP = NX * NY, NZ * NC
SIDE = 128
PIVOTS = 4
TILE = (8, 128)


def remote(src, dst, send_sem, recv_sem, device):
    return pltpu.make_async_remote_copy(
        src_ref=src, dst_ref=dst, send_sem=send_sem, recv_sem=recv_sem,
        device_id=device, device_id_type=MESH,
    )


def update_kernel(
    lm_hbm, basis_hbm, sens_hbm, blk_ref, obs_ref, noise_ref, pert_hbm,
    out_ref,
    lm_ref, basis_ref, sens_ref, pert_ref, in_sem, abuf, gram_ref, cross_ref,
    fbuf, sens_t, pred, dbuf, mbuf, sbuf, part, rbuf, tot, gbuf,
    xs_sem, xr_sem, ys_sem, yr_sem,
    ds_sem, dr_sem, ms_sem, mr_sem, dps_sem, dpr_sem, mps_sem, mpr_sem,
    rs_sem, rr_sem, as_sem, ar_sem, gs_sem, gr_sem, gps_sem, gpr_sem,
    fs_sem, fr_sem, fps_sem, fpr_sem,
):
    g = lax.axis_index("grp")
    v = lax.axis_index("vox")
    z, core = g // NC, g % NC
    x, y = v // NY, v % NY
    partner = z * NC + (1 - core)
    j_dev, vox_dev = lm_ref.shape
    block_vox, width = basis_ref.shape
    blocks_dev = vox_dev // block_vox
    n_obs = sens_ref.shape[0]
    half = n_obs // 2
    members = j_dev * N_GRP
    scale_root = math.sqrt(members - 1)

    fetches = [
        pltpu.make_async_copy(src, dst, in_sem.at[i])
        for i, (src, dst) in enumerate(
            ((lm_hbm, lm_ref), (basis_hbm, basis_ref), (sens_hbm, sens_ref), (pert_hbm, pert_ref))
        )
    ]
    for fetch in fetches:
        fetch.start()
    barrier = pltpu.get_barrier_semaphore()

    def greet_vox(i, _):
        pl.semaphore_signal(barrier, inc=1, device_id={"vox": (v + i) % N_VOX}, device_id_type=MESH)
        return 0

    def z_peer(i):
        return ((z + i) % NZ) * NC + core

    def greet_grp(i, _):
        pl.semaphore_signal(barrier, inc=1, device_id={"grp": z_peer(i)}, device_id_type=MESH)
        return 0

    lax.fori_loop(1, N_VOX, greet_vox, 0)
    lax.fori_loop(1, NZ, greet_grp, 0)
    pl.semaphore_signal(barrier, inc=1, device_id={"grp": partner}, device_id_type=MESH)

    fetches[0].wait()
    fetches[1].wait()
    lm = lm_ref[...]
    compliance = jnp.exp(-lm)
    stacked = jnp.concatenate(
        [compliance[:, b * block_vox : (b + 1) * block_vox] for b in range(blocks_dev)], axis=0
    ).astype(jnp.bfloat16)
    features = jnp.dot(stacked, basis_ref[...], preferred_element_type=jnp.float32)
    fbuf[y, x] = features.astype(jnp.bfloat16)
    lane_half = vox_dev // 2
    abuf[g] = jnp.concatenate([lm[:, :lane_half], lm[:, lane_half:]], axis=0).astype(jnp.bfloat16)
    pl.semaphore_wait(barrier, N_VOX - 1 + NZ - 1 + 1)

    z_last = NZ // 2

    def field_part(slot, way, step):
        if step < z_last:
            return abuf.at[slot]
        return abuf.at[slot, :, pl.ds(way * (lane_half // 2), lane_half // 2)]

    def field_copy(way, step, arriving):
        turn = 1 if way == 0 else NZ - 1
        back = step if arriving else step - 1
        slot = ((z + (NZ - turn) * back) % NZ) * NC + core
        ref = field_part(slot, way, step)
        return remote(ref, ref, fs_sem.at[way, step - 1], fr_sem.at[way, step - 1],
                      {"grp": ((z + turn) % NZ) * NC + core})

    def field_partner(i, arriving):
        slot = ((z + NZ - i) % NZ) * NC + (1 - core if arriving else core)
        return remote(abuf.at[slot], abuf.at[slot], fps_sem.at[i], fpr_sem.at[i], {"grp": partner})

    def field_step(step):
        for way in range(2):
            if step > 0:
                field_copy(way, step, True).wait_recv()
            if step < z_last:
                field_copy(way, step + 1, False).start()
        if step in (0, z_last):
            field_partner(step, False).start()
        else:
            field_partner(step, False).start()
            field_partner(NZ - step, False).start()

    def x_copy(i):
        src = (x + NX - i) % NX
        mine = remote(fbuf.at[y, x], fbuf.at[y, x], xs_sem.at[i], xr_sem.at[i],
                      {"vox": ((x + i) % NX) * NY + y})
        theirs = remote(fbuf.at[y, src], fbuf.at[y, src], xs_sem.at[i], xr_sem.at[i],
                        {"vox": ((x + i) % NX) * NY + y})
        return mine, theirs

    def y_copy(way, step, xi, arriving):
        turn = 1 if way == 0 else NY - 1
        xs = (x + xi) % NX
        back = step if arriving else step - 1
        ys = (y + (NY - turn) * back) % NY
        slot = fbuf.at[ys, xs]
        return remote(slot, slot, ys_sem.at[way, step - 1, xi], yr_sem.at[way, step - 1, xi],
                      {"vox": x * NY + (y + turn) % NY}), ys, xs

    def y_send(way, step, xi):
        y_copy(way, step, xi, False)[0].start()

    for i in (1, NX - 1, 2):
        x_copy(i)[0].start()
    y_send(0, 1, 0)
    y_send(1, 1, 0)
    field_step(0)
    fetches[2].wait()
    sens_t[...] = sens_ref[...].T
    pred[...] = jnp.zeros_like(pred)
    blk = blk_ref[...]

    def compute(ys, xs):
        all_pred = jnp.dot(fbuf[ys, xs], sens_t[...], preferred_element_type=jnp.float32)
        first = (xs * NY + ys) * blocks_dev
        acc = pred[...]
        for b in range(blocks_dev):
            acc = jnp.where(blk == first + b, all_pred[b * j_dev : (b + 1) * j_dev], acc)
        pred[...] = acc

    compute(y, x)

    def far(n):
        return n + n // 2 - 2 * (n // 3)

    def x_turn(n, _):
        xi = far(n)
        i = NX - xi
        x_copy(i)[1].wait_recv()
        y_send(0, 1, xi)
        y_send(1, 1, xi)
        compute(y, (x + xi) % NX)
        return 0

    lax.fori_loop(1, NX, x_turn, 0)
    last = NY // 2

    def y_turn(n, _):
        step, xi = n // NX + 1, far(n % NX)
        low = n % NX < NX // 2
        up, up_y, xs = y_copy(0, step, xi, True)
        up.wait_recv()

        @pl.when((step + 1 < last) | low)
        def _():
            y_send(0, step + 1, xi)

        down, down_y, _ = y_copy(1, step, xi, True)
        down.wait_recv()

        @pl.when((step + 1 < last) | jnp.logical_not(low))
        def _():
            y_send(1, step + 1, xi)

        compute(up_y, xs)
        compute(down_y, xs)
        return 0

    lax.fori_loop(0, 2 * NX, y_turn, 0)
    field_step(1)
    lax.fori_loop(2 * NX, (last - 1) * NX, y_turn, 0)

    def y_last(n, _):
        xi = far(n)

        @pl.when(n < NX // 2)
        def _():
            y_copy(0, last, xi, True)[0].wait_recv()

        @pl.when(n >= NX // 2)
        def _():
            y_copy(1, last, xi, True)[0].wait_recv()

        compute((y + last) % NY, (x + xi) % NX)
        return 0

    lax.fori_loop(0, NX, y_last, 0)

    own_pred = pred[...]
    own_mean = jnp.mean(own_pred, axis=0, keepdims=True)
    mbuf[g] = own_mean
    dev = own_pred - own_mean
    dbuf[g] = jnp.concatenate([dev[:, :half], dev[:, half:]], axis=0).astype(jnp.bfloat16)

    def peer_copies(i, arriving):
        slot = ((z + NZ - i) % NZ) * NC + core if arriving else g
        to = {"grp": z_peer(i)}
        return (remote(dbuf.at[slot], dbuf.at[slot], ds_sem.at[i], dr_sem.at[i], to),
                remote(mbuf.at[slot], mbuf.at[slot], ms_sem.at[i], mr_sem.at[i], to))

    def partner_copies(i, arriving):
        slot = ((z + NZ - i) % NZ) * NC + (1 - core if arriving else core)
        to = {"grp": partner}
        return (remote(dbuf.at[slot], dbuf.at[slot], dps_sem.at[i], dpr_sem.at[i], to),
                remote(mbuf.at[slot], mbuf.at[slot], mps_sem.at[i], mpr_sem.at[i], to))

    def send_peer(i, _):
        for copy in peer_copies(i, False):
            copy.start()
        return 0

    def forward(i, _):
        for copy in peer_copies(i, True):
            copy.wait_recv()
        for copy in partner_copies(i, False):
            copy.start()
        return 0

    def from_partner(i, _):
        for copy in partner_copies(i, True):
            copy.wait_recv()
        return 0

    lax.fori_loop(1, NZ, send_peer, 0)
    for copy in partner_copies(0, False):
        copy.start()
    noise = noise_ref[...]
    scale = 1.0 / (noise * scale_root)
    fetches[3].wait()
    misfit = ((obs_ref[...] - own_pred) / noise + pert_ref[...]).astype(jnp.bfloat16)
    misfit_wide = misfit.astype(jnp.float32)
    squares = misfit_wide * misfit_wide
    lax.fori_loop(1, NZ, forward, 0)
    lax.fori_loop(0, NZ, from_partner, 0)

    centre = jnp.sum(mbuf[...], axis=0) * (1.0 / N_GRP)

    def scaled_of(group):
        d = dbuf[group].astype(jnp.float32)
        wide = jnp.concatenate([d[:j_dev], d[j_dev:]], axis=1)
        return (wide + (mbuf[group] - centre)) * scale

    def scale_pair(n, _):
        both = jnp.concatenate([scaled_of(2 * n), scaled_of(2 * n + 1)], axis=0)
        rows = 2 * j_dev
        sbuf[pl.ds(pl.multiple_of(n * rows, 16), rows), :] = both.astype(jnp.bfloat16)
        return 0

    lax.fori_loop(0, NZ, scale_pair, 0)
    left = jnp.concatenate([scaled_of(g), misfit_wide], axis=0).astype(jnp.bfloat16)
    sums = lax.dot_general(left, sbuf[...], (((1,), (1,)), ((), ())), preferred_element_type=jnp.float32)

    n_row, n_col = j_dev // 8, members // 128
    n_gram = n_row * n_col
    n_tiles = 2 * n_gram + 1
    for h in range(2):
        for i in range(n_row):
            for c in range(n_col):
                t = h * (n_gram + 1) + i * n_col + c
                part[t] = sums[h * j_dev + 8 * i : h * j_dev + 8 * i + 8, 128 * c : 128 * c + 128]
    folded = squares[0:8]
    for i in range(1, n_row):
        folded = folded + squares[8 * i : 8 * i + 8]
    lanes = folded[:, 0:128]
    for c in range(1, n_obs // 128):
        lanes = lanes + folded[:, 128 * c : 128 * c + 128]
    part[n_gram] = lanes

    def send_part(i, _):
        t = (v + i) % n_tiles

        @pl.when(t != v)
        def _():
            remote(part.at[t], rbuf.at[v], rs_sem, rr_sem, {"vox": t}).start()

        return 0

    lax.fori_loop(0, n_tiles, send_part, 0)
    field_step(2)

    @pl.when(v < n_tiles)
    def _():
        rbuf[v] = part[v]
        got = rbuf.at[pl.ds(0, N_VOX - 1)]
        pltpu.make_async_copy(got, got, rr_sem).wait()
        tot[v] = jnp.sum(rbuf[...], axis=0)

        def spread(i, _):
            remote(tot.at[v], tot.at[v], as_sem, ar_sem, {"vox": (v + i) % N_VOX}).start()
            return 0

        lax.fori_loop(1, N_VOX, spread, 0)
        most = tot.at[pl.ds(0, n_tiles - 1)]
        pltpu.make_async_copy(most, most, ar_sem).wait()

    @pl.when(v >= n_tiles)
    def _():
        whole = tot.at[pl.ds(0, n_tiles)]
        pltpu.make_async_copy(whole, whole, ar_sem).wait()

    gbuf[g] = tot[0 : n_gram + 1]

    def rows_copy(i, arriving):
        slot = gbuf.at[((z + NZ - i) % NZ) * NC + core if arriving else g]
        return remote(slot, slot, gs_sem.at[i], gr_sem.at[i], {"grp": z_peer(i)})

    def rows_partner(i, arriving):
        slot = gbuf.at[((z + NZ - i) % NZ) * NC + (1 - core if arriving else core)]
        return remote(slot, slot, gps_sem.at[i], gpr_sem.at[i], {"grp": partner})

    def rows_send(i, _):
        rows_copy(i, False).start()
        return 0

    def rows_forward(i, _):
        rows_copy(i, True).wait_recv()
        rows_partner(i, False).start()
        return 0

    def rows_from(i, _):
        rows_partner(i, True).wait_recv()
        return 0

    lax.fori_loop(1, NZ, rows_send, 0)
    rows_partner(0, False).start()
    for i in range(n_row):
        for c in range(n_col):
            cross_ref[8 * i : 8 * i + 8, 128 * c : 128 * c + 128] = tot[n_gram + 1 + i * n_col + c]
    lax.fori_loop(1, NZ, rows_forward, 0)
    lax.fori_loop(0, NZ, rows_from, 0)

    def place(n, _):
        for i in range(n_row):
            row = pl.multiple_of(n * j_dev + 8 * i, 8)
            for c in range(n_col):
                gram_ref[pl.ds(row, 8), 128 * c : 128 * c + 128] = gbuf[n, i * n_col + c]
        return 0

    lax.fori_loop(0, N_GRP, place, 0)
    squares_all = jnp.sum(gbuf[:, n_gram], axis=0)
    damping = jnp.sum(squares_all, keepdims=True) * (1.0 / (members * n_obs * N_VOX))
    field_step(3)
    weights = solve(gram_ref, cross_ref, damping, lambda: field_step(z_last)).astype(jnp.bfloat16)

    def field_from(i, _):
        field_partner(i, True).wait_recv()
        return 0

    lax.fori_loop(0, NZ, field_from, 0)
    col = lax.broadcasted_iota(jnp.int32, (members, 2 * members), 1)
    row = lax.broadcasted_iota(jnp.int32, (members, 2 * members), 0)
    group = jnp.floor((row.astype(jnp.float32) + 0.5) * (1.0 / j_dev)).astype(jnp.int32)
    place_of = row + group * j_dev
    spread_weights = jnp.concatenate(
        [
            jnp.dot(weights, (col == place_of + j_dev * h).astype(jnp.bfloat16),
                    preferred_element_type=jnp.float32)
            for h in range(2)
        ],
        axis=0,
    ).astype(jnp.bfloat16)
    piece = 512
    for n in range(lane_half // piece):
        cut = slice(n * piece, (n + 1) * piece)
        field = abuf[:, :, cut].reshape(2 * members, piece)
        mixture = jnp.dot(spread_weights, field, preferred_element_type=jnp.float32) * (1.0 / scale_root)
        for h in range(2):
            cols = slice(h * lane_half + n * piece, h * lane_half + (n + 1) * piece)
            out_ref[:, cols] = lm_ref[:, cols] + mixture[h * j_dev : (h + 1) * j_dev]

    for i in range(1, NX):
        x_copy(i)[0].wait_send()

    def y_sent(n, _):
        step, xi = n // NX + 1, far(n % NX)
        low = n % NX < NX // 2

        @pl.when((step < last) | low)
        def _():
            y_copy(0, step, xi, False)[0].wait_send()

        @pl.when((step < last) | jnp.logical_not(low))
        def _():
            y_copy(1, step, xi, False)[0].wait_send()

        return 0

    lax.fori_loop(0, last * NX, y_sent, 0)

    def grp_sent(i, _):
        for copy in (*peer_copies(i, False), rows_copy(i, False)):
            copy.wait_send()
        return 0

    def partner_sent(i, _):
        for copy in (*partner_copies(i, False), rows_partner(i, False), field_partner(i, False)):
            copy.wait_send()
        return 0

    lax.fori_loop(1, NZ, grp_sent, 0)
    lax.fori_loop(0, NZ, partner_sent, 0)
    for way in range(2):
        for step in range(1, z_last + 1):
            field_copy(way, step, False).wait_send()

    @pl.when(v < n_tiles)
    def _():
        sent = part.at[pl.ds(0, n_tiles - 1)]
        pltpu.make_async_copy(sent, sent, rs_sem).wait()
        spread_all = rbuf.at[pl.ds(0, N_VOX - 1)]
        pltpu.make_async_copy(spread_all, spread_all, as_sem).wait()

    @pl.when(v >= n_tiles)
    def _():
        sent = part.at[pl.ds(0, n_tiles)]
        pltpu.make_async_copy(sent, sent, rs_sem).wait()


def update(log_modulus, basis, sensitivity, blocks, observed, noise, perturbation):
    j_dev, vox_dev = log_modulus.shape
    block_vox, width = basis.shape
    blocks_dev = vox_dev // block_vox
    n_obs = sensitivity.shape[0]
    members = j_dev * N_GRP
    n_gram = (j_dev // 8) * (members // 128)
    n_tiles = 2 * n_gram + 1
    f32, bf16 = jnp.float32, jnp.bfloat16
    dma = pltpu.SemaphoreType.DMA
    vmem = pl.BlockSpec(memory_space=pltpu.VMEM)
    hbm = pl.BlockSpec(memory_space=pltpu.HBM)
    return pl.pallas_call(
        update_kernel,
        out_shape=jax.ShapeDtypeStruct((j_dev, vox_dev), f32),
        in_specs=[hbm, hbm, hbm, vmem, vmem, vmem, hbm],
        out_specs=vmem,
        scratch_shapes=[
            pltpu.VMEM((j_dev, vox_dev), f32),
            pltpu.VMEM((block_vox, width), bf16),
            pltpu.VMEM((n_obs, width), bf16),
            pltpu.VMEM((j_dev, n_obs), f32),
            dma((4,)),
            pltpu.VMEM((N_GRP, 2 * j_dev, vox_dev // 2), bf16),
            pltpu.VMEM((members, members), f32),
            pltpu.VMEM((j_dev, members), f32),
            pltpu.VMEM((NY, NX, blocks_dev * j_dev, width), bf16),
            pltpu.VMEM((width, n_obs), bf16),
            pltpu.VMEM((j_dev, n_obs), f32),
            pltpu.VMEM((N_GRP, 2 * j_dev, n_obs // 2), bf16),
            pltpu.VMEM((N_GRP, 1, n_obs), f32),
            pltpu.VMEM((members, n_obs), bf16),
            pltpu.VMEM((n_tiles, *TILE), f32),
            pltpu.VMEM((N_VOX, *TILE), f32),
            pltpu.VMEM((n_tiles, *TILE), f32),
            pltpu.VMEM((N_GRP, n_gram + 1, *TILE), f32),
            dma((NX,)), dma((NX,)), dma((2, NY // 2, NX)), dma((2, NY // 2, NX)),
            dma((NZ,)), dma((NZ,)), dma((NZ,)), dma((NZ,)),
            dma((NZ,)), dma((NZ,)), dma((NZ,)), dma((NZ,)),
            dma, dma, dma, dma,
            dma((NZ,)), dma((NZ,)), dma((NZ,)), dma((NZ,)),
            dma((2, NZ // 2)), dma((2, NZ // 2)), dma((NZ,)), dma((NZ,)),
        ],
        compiler_params=pltpu.CompilerParams(
            collective_id=0, has_side_effects=True, vmem_limit_bytes=62 << 20
        ),
        name="update",
    )(log_modulus, basis, sensitivity, blocks, observed, noise, perturbation)


def product(a, b):
    return lax.dot_general(
        a, b, (((1,), (0,)), ((), ())), precision=HIGHEST, preferred_element_type=jnp.float32
    )


def inverse(d, k):
    n = d.shape[0]
    lane = lax.broadcasted_iota(jnp.int32, (1, n), 1)
    sub = lax.broadcasted_iota(jnp.int32, (n, 1), 0)
    for p in range(0, n, k):
        cols = [jnp.broadcast_to(d[:, p + j : p + j + 1], (n, n)) for j in range(k)]
        s = [[cols[j][p + i : p + i + 1] for j in range(k)] for i in range(k)]
        inside = (lane >= p) & (lane < p + k)
        rows = [
            jnp.where(inside, (lane == p + i).astype(jnp.float32), d[p + i : p + i + 1])
            for i in range(k)
        ]
        for i in range(k):
            inv = 1.0 / s[i][i]
            rows[i] = rows[i] * inv
            for j in range(i + 1, k):
                s[i][j] = s[i][j] * inv
            for r in range(k):
                if r != i:
                    rows[r] = rows[r] - s[r][i] * rows[i]
                    for j in range(i + 1, k):
                        s[r][j] = s[r][j] - s[r][i] * s[i][j]
        row_in = (sub >= p) & (sub < p + k)
        d = jnp.where(inside | row_in, 0.0, d)
        for j in range(k):
            d = d - jnp.where(row_in, jnp.where(sub == p + j, -1.0, 0.0), cols[j]) * rows[j]
    return d


def solve(gram_ref, cross_ref, damp, between):
    b = SIDE
    eye = lax.broadcasted_iota(jnp.int32, (b, b), 0) == lax.broadcasted_iota(jnp.int32, (b, b), 1)

    def block(i, j):
        found = gram_ref[i * b : (i + 1) * b, j * b : (j + 1) * b]
        return found + jnp.where(eye, damp, 0.0) if i == j else found

    c0, c1, c2 = (cross_ref[:, i * b : (i + 1) * b] for i in range(3))
    a01, a02, a12 = block(0, 1), block(0, 2), block(1, 2)
    a10, a20, a21 = block(1, 0), block(2, 0), block(2, 1)
    i0 = inverse(block(0, 0), PIVOTS)
    u01 = product(i0, a01)
    u02 = product(i0, a02)
    y0 = product(c0, i0)
    i1 = inverse(block(1, 1) - product(a10, u01), PIVOTS)
    a12 = a12 - product(a10, u02)
    a21 = a21 - product(a20, u01)
    a22 = block(2, 2) - product(a20, u02)
    z1 = c1 - product(y0, a01)
    z2 = c2 - product(y0, a02)
    between()
    u12 = product(i1, a12)
    y1 = product(z1, i1)
    i2 = inverse(a22 - product(a21, u12), PIVOTS)
    z2 = z2 - product(y1, a12)
    x2 = product(z2, i2)
    x1 = product(z1 - product(x2, a21), i1)
    x0 = product(c0 - product(x1, a10) - product(x2, a20), i0)
    return jnp.concatenate([x0, x1, x2], axis=1)


def on_device(log_modulus, basis, sensitivity, obs_block, observed, noise_scale, perturbation):
    n_obs = sensitivity.shape[0]
    return update(
        log_modulus, basis, sensitivity, obs_block.reshape(1, n_obs),
        observed.reshape(1, n_obs), noise_scale.reshape(1, n_obs), perturbation,
    )


def solution(mesh):
    in_specs = (
        P("grp", "vox"), P(), P("vox", None), P("vox", None), P("vox"), P("vox"), P("grp", "vox"),
    )
    return jax.shard_map(
        on_device, mesh=mesh, in_specs=in_specs, out_specs=P("grp", "vox"), check_vma=False
    )
```

```python
import functools
import math

import jax
import jax.numpy as jnp
from jax import lax
from jax.experimental import pallas as pl
from jax.experimental.pallas import tpu as pltpu
from jax.sharding import PartitionSpec as P

MESH = pl.DeviceIdType.MESH
HIGHEST = lax.Precision.HIGHEST
NX, NY, NZ, NC = 4, 8, 8, 2
N_VOX, N_GRP = NX * NY, NZ * NC
SIDE = 128
PIVOTS = 4
TILE = (8, 128)
CAP = 8
ROWS = 16


def remote(src, dst, send_sem, recv_sem, device):
    return pltpu.make_async_remote_copy(
        src_ref=src, dst_ref=dst, send_sem=send_sem, recv_sem=recv_sem,
        device_id=device, device_id_type=MESH,
    )


def update_kernel(
    lm_hbm, basis_hbm, sens_hbm, blk_ref, obs_ref, noise_ref, pert_hbm,
    out_ref,
    lm_ref, basis_ref, sens_ref, pert_ref, in_sem, abuf, gram_ref, cross_ref,
    xout, xin, pbuf, phi, pred_ref, part, rbuf, tot, gbuf,
    xs_sem, xr_sem, ds_sem, dr_sem, dps_sem, dpr_sem,
    rs_sem, rr_sem, as_sem, ar_sem, gs_sem, gr_sem, gps_sem, gpr_sem,
    fs_sem, fr_sem, fps_sem, fpr_sem,
):
    g = lax.axis_index("grp")
    v = lax.axis_index("vox")
    z, core = g // NC, g % NC
    x, y = v // NY, v % NY
    partner = z * NC + (1 - core)
    j_dev, vox_dev = lm_ref.shape
    block_vox, width = basis_ref.shape
    blocks_dev = vox_dev // block_vox
    n_obs = sens_ref.shape[0]
    members = j_dev * N_GRP
    scale_root = math.sqrt(members - 1)

    in_blocks = [slice(b * block_vox, (b + 1) * block_vox) for b in range(blocks_dev)]
    pairs = [(lm_hbm.at[:, cut], lm_ref.at[:, cut]) for cut in in_blocks]
    pairs += [(basis_hbm, basis_ref), (sens_hbm, sens_ref), (pert_hbm, pert_ref)]
    fetches = [pltpu.make_async_copy(src, dst, in_sem.at[i]) for i, (src, dst) in enumerate(pairs)]
    for fetch in fetches:
        fetch.start()
    barrier = pltpu.get_barrier_semaphore()

    def greet_vox(i, _):
        pl.semaphore_signal(barrier, inc=1, device_id={"vox": (v + i) % N_VOX}, device_id_type=MESH)
        return 0

    def z_peer(i):
        return ((z + i) % NZ) * NC + core

    def greet_grp(i, _):
        pl.semaphore_signal(barrier, inc=1, device_id={"grp": z_peer(i)}, device_id_type=MESH)
        return 0

    lax.fori_loop(1, N_VOX, greet_vox, 0)
    lax.fori_loop(1, NZ, greet_grp, 0)
    pl.semaphore_signal(barrier, inc=1, device_id={"grp": partner}, device_id_type=MESH)

    strips = []
    for b in range(blocks_dev):
        fetches[b].wait()
        strips.append(jnp.exp(-lm_ref[:, in_blocks[b]]))
    stacked = jnp.concatenate(strips, axis=0).astype(jnp.bfloat16)
    fetches[blocks_dev].wait()
    features = jnp.dot(stacked, basis_ref[...], preferred_element_type=jnp.float32)
    wide = jnp.concatenate([features[b * j_dev : (b + 1) * j_dev] for b in range(blocks_dev)], axis=1)
    f_half = blocks_dev * width // 2
    pbuf[g] = jnp.concatenate([wide[:, :f_half], wide[:, f_half:]], axis=0).astype(jnp.bfloat16)
    lane_half = vox_dev // 2
    pl.semaphore_wait(barrier, N_VOX - 1 + NZ - 1 + 1)

    def peer_copy(i, arriving):
        slot = pbuf.at[((z + NZ - i) % NZ) * NC + core if arriving else g]
        return remote(slot, slot, ds_sem.at[i], dr_sem.at[i], {"grp": z_peer(i)})

    def partner_copy(i, arriving):
        slot = pbuf.at[((z + NZ - i) % NZ) * NC + (1 - core if arriving else core)]
        return remote(slot, slot, dps_sem.at[i], dpr_sem.at[i], {"grp": partner})

    def send_peer(i, _):
        peer_copy(i, False).start()
        return 0

    def forward(i, _):
        peer_copy(i, True).wait_recv()
        partner_copy(i, False).start()
        return 0

    def from_partner(i, _):
        partner_copy(i, True).wait_recv()
        return 0

    lax.fori_loop(1, NZ, send_peer, 0)
    partner_copy(0, False).start()

    z_last = NZ // 2

    def field_part(slot, way, step):
        if step < z_last:
            return abuf.at[slot]
        return abuf.at[slot, :, pl.ds(way * (lane_half // 2), lane_half // 2)]

    def field_copy(way, step, arriving):
        turn = 1 if way == 0 else NZ - 1
        back = step if arriving else step - 1
        slot = ((z + (NZ - turn) * back) % NZ) * NC + core
        ref = field_part(slot, way, step)
        return remote(ref, ref, fs_sem.at[way, step - 1], fr_sem.at[way, step - 1],
                      {"grp": ((z + turn) % NZ) * NC + core})

    def field_partner(i, arriving):
        slot = ((z + NZ - i) % NZ) * NC + (1 - core if arriving else core)
        return remote(abuf.at[slot], abuf.at[slot], fps_sem.at[i], fpr_sem.at[i], {"grp": partner})

    def field_step(step):
        for way in range(2):
            if step > 0:
                field_copy(way, step, True).wait_recv()
            if step < z_last:
                field_copy(way, step + 1, False).start()
        if step in (0, z_last):
            field_partner(step, False).start()
        else:
            field_partner(step, False).start()
            field_partner(NZ - step, False).start()

    n_blocks = blocks_dev * N_VOX
    slots = blocks_dev * CAP
    groups = slots // ROWS
    blk = blk_ref[...]
    hit = (lax.broadcasted_iota(jnp.int32, (n_blocks, n_obs), 0) == blk).astype(jnp.float32)
    before = (
        lax.broadcasted_iota(jnp.int32, (n_obs, n_obs), 0)
        < lax.broadcasted_iota(jnp.int32, (n_obs, n_obs), 1)
    ).astype(jnp.float32)
    counts = jnp.dot(
        hit.astype(jnp.bfloat16), before.astype(jnp.bfloat16), preferred_element_type=jnp.float32
    )
    rank = jnp.sum(hit * counts, axis=0, keepdims=True)
    slot_of = blk * CAP + rank.astype(jnp.int32)

    def three(value):
        first = value.astype(jnp.bfloat16).astype(jnp.float32)
        second = (value - first).astype(jnp.bfloat16).astype(jnp.float32)
        return first, second, value - first - second

    observed = obs_ref[...]
    sub = lax.broadcasted_iota(jnp.int32, (8, n_obs), 0)
    tail = jnp.zeros((8, n_obs), jnp.float32)
    for i, term in enumerate((*three(observed), *three(1.0 / noise_ref[...]))):
        tail = jnp.where(sub == i, term, tail)
    fetches[blocks_dev + 1].wait()
    fetches[blocks_dev + 2].wait()
    with_obs = jnp.concatenate([pert_ref[...], tail], axis=0).astype(jnp.bfloat16)
    row_id = lax.broadcasted_iota(jnp.int32, (N_VOX * ROWS, n_obs), 0)
    code = row_id + (slots - ROWS) * lax.shift_right_logical(row_id, ROWS.bit_length() - 1)
    extras = []
    for q in range(groups):
        take = (code == slot_of - ROWS * q).astype(jnp.float32).astype(jnp.bfloat16)
        rows_q = jnp.dot(take, sens_ref[...], preferred_element_type=jnp.float32)
        xout[:, ROWS * q : ROWS * (q + 1), :] = rows_q.astype(jnp.bfloat16).reshape(N_VOX, ROWS, width)
        extras.append(
            lax.dot_general(take, with_obs, (((1,), (1,)), ((), ())), preferred_element_type=jnp.float32)
        )
    beside = jnp.concatenate(extras, axis=1).astype(jnp.bfloat16)
    xout[:, slots : slots + ROWS, :] = beside.reshape(N_VOX, ROWS, width)

    def send_rows(i, _):
        to = (v + i) % N_VOX
        remote(xout.at[to], xin.at[v], xs_sem, xr_sem, {"vox": to}).start()
        return 0

    lax.fori_loop(1, N_VOX, send_rows, 0)
    xin[v] = xout[v]
    lm = lm_ref[...]
    abuf[g] = jnp.concatenate([lm[:, :lane_half], lm[:, lane_half:]], axis=0).astype(jnp.bfloat16)
    field_step(0)
    lax.fori_loop(1, NZ, forward, 0)
    lax.fori_loop(0, NZ, from_partner, 0)

    def features_of(group):
        d = pbuf[group].astype(jnp.float32)
        return jnp.concatenate([d[:j_dev], d[j_dev:]], axis=1)

    def place_pair(n, _):
        both = jnp.concatenate([features_of(2 * n), features_of(2 * n + 1)], axis=0)
        rows = 2 * j_dev
        phi[pl.ds(pl.multiple_of(n * rows, 16), rows), :] = both.astype(jnp.bfloat16)
        return 0

    lax.fori_loop(0, NZ, place_pair, 0)
    field_step(1)
    got_rows = xin.at[pl.ds(0, N_VOX - 1)]
    pltpu.make_async_copy(got_rows, got_rows, xr_sem).wait()

    n_here = N_VOX * ROWS
    extra = xin[:, slots : slots + ROWS, :].astype(jnp.float32).reshape(n_here, width).T
    per = width // groups
    low = (lax.broadcasted_iota(jnp.int32, (n_here, width), 0) & (ROWS - 1)) < CAP
    sums = jnp.zeros((2 * j_dev, members), jnp.float32)
    lanes = jnp.zeros(TILE, jnp.float32)
    pair = 2 * width
    contract = (((1,), (1,)), ((), ()))
    for q in range(groups):
        rows_q = xin[:, ROWS * q : ROWS * (q + 1), :].astype(jnp.float32).reshape(n_here, width)
        both = jnp.concatenate([jnp.where(low, rows_q, 0.0), jnp.where(low, 0.0, rows_q)], axis=1)
        pred = lax.dot_general(
            phi[:, pair * q : pair * (q + 1)], both.astype(jnp.bfloat16), contract,
            preferred_element_type=jnp.float32,
        )
        pred_ref[...] = pred
        centre = jnp.sum(pred, axis=0, keepdims=True) * (1.0 / members)
        at = per * q + j_dev
        seen = extra[at : at + 1] + extra[at + 1 : at + 2] + extra[at + 2 : at + 3]
        inv_noise = extra[at + 3 : at + 4] + extra[at + 4 : at + 5] + extra[at + 5 : at + 6]
        scale = inv_noise * (1.0 / scale_root)
        scaled = ((pred - centre) * scale).astype(jnp.bfloat16)
        own_pred = pred_ref[pl.ds(pl.multiple_of(g * j_dev, 8), j_dev), :]
        misfit = (seen - own_pred) * inv_noise + extra[per * q : per * q + j_dev]
        misfit = misfit.astype(jnp.bfloat16).astype(jnp.float32)
        left = jnp.concatenate([(own_pred - centre) * scale, misfit], axis=0).astype(jnp.bfloat16)
        sums = sums + lax.dot_general(left, scaled, contract, preferred_element_type=jnp.float32)
        squares = misfit * misfit
        for i in range(j_dev // 8):
            for c in range(n_here // 128):
                lanes = lanes + squares[8 * i : 8 * i + 8, 128 * c : 128 * c + 128]

    n_row, n_col = j_dev // 8, members // 128
    n_gram = n_row * n_col
    n_tiles = 2 * n_gram + 1
    for h in range(2):
        for i in range(n_row):
            for c in range(n_col):
                t = h * (n_gram + 1) + i * n_col + c
                part[t] = sums[h * j_dev + 8 * i : h * j_dev + 8 * i + 8, 128 * c : 128 * c + 128]
    part[n_gram] = lanes

    def send_part(i, _):
        t = (v + i) % n_tiles

        @pl.when(t != v)
        def _():
            remote(part.at[t], rbuf.at[v], rs_sem, rr_sem, {"vox": t}).start()

        return 0

    lax.fori_loop(0, n_tiles, send_part, 0)
    field_step(2)

    @pl.when(v < n_tiles)
    def _():
        rbuf[v] = part[v]
        got = rbuf.at[pl.ds(0, N_VOX - 1)]
        pltpu.make_async_copy(got, got, rr_sem).wait()
        tot[v] = jnp.sum(rbuf[...], axis=0)

        def spread(i, _):
            remote(tot.at[v], tot.at[v], as_sem, ar_sem, {"vox": (v + i) % N_VOX}).start()
            return 0

        lax.fori_loop(1, N_VOX, spread, 0)
        most = tot.at[pl.ds(0, n_tiles - 1)]
        pltpu.make_async_copy(most, most, ar_sem).wait()

    @pl.when(v >= n_tiles)
    def _():
        whole = tot.at[pl.ds(0, n_tiles)]
        pltpu.make_async_copy(whole, whole, ar_sem).wait()

    gbuf[g] = tot[0 : n_gram + 1]

    def rows_copy(i, arriving):
        slot = gbuf.at[((z + NZ - i) % NZ) * NC + core if arriving else g]
        return remote(slot, slot, gs_sem.at[i], gr_sem.at[i], {"grp": z_peer(i)})

    def rows_partner(i, arriving):
        slot = gbuf.at[((z + NZ - i) % NZ) * NC + (1 - core if arriving else core)]
        return remote(slot, slot, gps_sem.at[i], gpr_sem.at[i], {"grp": partner})

    def rows_send(i, _):
        rows_copy(i, False).start()
        return 0

    def rows_forward(i, _):
        rows_copy(i, True).wait_recv()
        rows_partner(i, False).start()
        return 0

    def rows_from(i, _):
        rows_partner(i, True).wait_recv()
        return 0

    lax.fori_loop(1, NZ, rows_send, 0)
    rows_partner(0, False).start()
    for i in range(n_row):
        for c in range(n_col):
            cross_ref[8 * i : 8 * i + 8, 128 * c : 128 * c + 128] = tot[n_gram + 1 + i * n_col + c]
    lax.fori_loop(1, NZ, rows_forward, 0)
    lax.fori_loop(0, NZ, rows_from, 0)

    def place(n, _):
        for i in range(n_row):
            row = pl.multiple_of(n * j_dev + 8 * i, 8)
            for c in range(n_col):
                gram_ref[pl.ds(row, 8), 128 * c : 128 * c + 128] = gbuf[n, i * n_col + c]
        return 0

    lax.fori_loop(0, N_GRP, place, 0)
    squares_all = jnp.sum(gbuf[:, n_gram], axis=0)
    damping = jnp.sum(squares_all, keepdims=True) * (1.0 / (members * n_obs * N_VOX))
    field_step(3)
    weights = solve(gram_ref, cross_ref, damping, lambda: field_step(z_last)).astype(jnp.bfloat16)

    def field_from(i, _):
        field_partner(i, True).wait_recv()
        return 0

    lax.fori_loop(0, NZ, field_from, 0)
    col = lax.broadcasted_iota(jnp.int32, (members, 2 * members), 1)
    row = lax.broadcasted_iota(jnp.int32, (members, 2 * members), 0)
    group = jnp.floor((row.astype(jnp.float32) + 0.5) * (1.0 / j_dev)).astype(jnp.int32)
    place_of = row + group * j_dev
    spread_weights = jnp.concatenate(
        [
            jnp.dot(weights, (col == place_of + j_dev * h).astype(jnp.bfloat16),
                    preferred_element_type=jnp.float32)
            for h in range(2)
        ],
        axis=0,
    ).astype(jnp.bfloat16)
    piece = 512
    for n in range(lane_half // piece):
        cut = slice(n * piece, (n + 1) * piece)
        field = abuf[:, :, cut].reshape(2 * members, piece)
        mixture = jnp.dot(spread_weights, field, preferred_element_type=jnp.float32) * (1.0 / scale_root)
        for h in range(2):
            cols = slice(h * lane_half + n * piece, h * lane_half + (n + 1) * piece)
            out_ref[:, cols] = mixture[h * j_dev : (h + 1) * j_dev]

    sent_rows = xout.at[pl.ds(0, N_VOX - 1)]
    pltpu.make_async_copy(sent_rows, sent_rows, xs_sem).wait()

    def grp_sent(i, _):
        peer_copy(i, False).wait_send()
        rows_copy(i, False).wait_send()
        return 0

    def partner_sent(i, _):
        for copy in (partner_copy(i, False), rows_partner(i, False), field_partner(i, False)):
            copy.wait_send()
        return 0

    lax.fori_loop(1, NZ, grp_sent, 0)
    lax.fori_loop(0, NZ, partner_sent, 0)
    for way in range(2):
        for step in range(1, z_last + 1):
            field_copy(way, step, False).wait_send()

    @pl.when(v < n_tiles)
    def _():
        sent = part.at[pl.ds(0, n_tiles - 1)]
        pltpu.make_async_copy(sent, sent, rs_sem).wait()
        spread_all = rbuf.at[pl.ds(0, N_VOX - 1)]
        pltpu.make_async_copy(spread_all, spread_all, as_sem).wait()

    @pl.when(v >= n_tiles)
    def _():
        sent = part.at[pl.ds(0, n_tiles)]
        pltpu.make_async_copy(sent, sent, rs_sem).wait()


def update(log_modulus, basis, sensitivity, blocks, observed, noise, perturbation):
    j_dev, vox_dev = log_modulus.shape
    block_vox, width = basis.shape
    blocks_dev = vox_dev // block_vox
    n_obs = sensitivity.shape[0]
    members = j_dev * N_GRP
    n_gram = (j_dev // 8) * (members // 128)
    n_tiles = 2 * n_gram + 1
    f32, bf16 = jnp.float32, jnp.bfloat16
    dma = pltpu.SemaphoreType.DMA
    vmem = pl.BlockSpec(memory_space=pltpu.VMEM)
    hbm = pl.BlockSpec(memory_space=pltpu.HBM)
    return pl.pallas_call(
        update_kernel,
        out_shape=jax.ShapeDtypeStruct((j_dev, vox_dev), f32),
        in_specs=[hbm, hbm, hbm, vmem, vmem, vmem, hbm],
        out_specs=vmem,
        scratch_shapes=[
            pltpu.VMEM((j_dev, vox_dev), f32),
            pltpu.VMEM((block_vox, width), bf16),
            pltpu.VMEM((n_obs, width), bf16),
            pltpu.VMEM((j_dev, n_obs), f32),
            dma((blocks_dev + 3,)),
            pltpu.VMEM((N_GRP, 2 * j_dev, vox_dev // 2), bf16),
            pltpu.VMEM((members, members), f32),
            pltpu.VMEM((j_dev, members), f32),
            pltpu.VMEM((N_VOX, blocks_dev * CAP + ROWS, width), bf16),
            pltpu.VMEM((N_VOX, blocks_dev * CAP + ROWS, width), bf16),
            pltpu.VMEM((N_GRP, 2 * j_dev, blocks_dev * width // 2), bf16),
            pltpu.VMEM((members, blocks_dev * width), bf16),
            pltpu.VMEM((members, N_VOX * ROWS), f32),
            pltpu.VMEM((n_tiles, *TILE), f32),
            pltpu.VMEM((N_VOX, *TILE), f32),
            pltpu.VMEM((n_tiles, *TILE), f32),
            pltpu.VMEM((N_GRP, n_gram + 1, *TILE), f32),
            dma, dma, dma((NZ,)), dma((NZ,)), dma((NZ,)), dma((NZ,)),
            dma, dma, dma, dma,
            dma((NZ,)), dma((NZ,)), dma((NZ,)), dma((NZ,)),
            dma((2, NZ // 2)), dma((2, NZ // 2)), dma((NZ,)), dma((NZ,)),
        ],
        compiler_params=pltpu.CompilerParams(
            collective_id=0, has_side_effects=True, vmem_limit_bytes=62 << 20
        ),
        name="update",
    )(log_modulus, basis, sensitivity, blocks, observed, noise, perturbation)


def product(a, b):
    return lax.dot_general(
        a, b, (((1,), (0,)), ((), ())), precision=HIGHEST, preferred_element_type=jnp.float32
    )


def inverse(d, k):
    n = d.shape[0]
    lane = lax.broadcasted_iota(jnp.int32, (1, n), 1)
    sub = lax.broadcasted_iota(jnp.int32, (n, 1), 0)
    for p in range(0, n, k):
        cols = [jnp.broadcast_to(d[:, p + j : p + j + 1], (n, n)) for j in range(k)]
        s = [[cols[j][p + i : p + i + 1] for j in range(k)] for i in range(k)]
        inside = (lane >= p) & (lane < p + k)
        rows = [
            jnp.where(inside, (lane == p + i).astype(jnp.float32), d[p + i : p + i + 1])
            for i in range(k)
        ]
        for i in range(k):
            inv = 1.0 / s[i][i]
            rows[i] = rows[i] * inv
            for j in range(i + 1, k):
                s[i][j] = s[i][j] * inv
            for r in range(k):
                if r != i:
                    rows[r] = rows[r] - s[r][i] * rows[i]
                    for j in range(i + 1, k):
                        s[r][j] = s[r][j] - s[r][i] * s[i][j]
        row_in = (sub >= p) & (sub < p + k)
        d = jnp.where(inside | row_in, 0.0, d)
        for j in range(k):
            d = d - jnp.where(row_in, jnp.where(sub == p + j, -1.0, 0.0), cols[j]) * rows[j]
    return d


def solve(gram_ref, cross_ref, damp, between):
    b = SIDE
    eye = lax.broadcasted_iota(jnp.int32, (b, b), 0) == lax.broadcasted_iota(jnp.int32, (b, b), 1)

    def block(i, j):
        found = gram_ref[i * b : (i + 1) * b, j * b : (j + 1) * b]
        return found + jnp.where(eye, damp, 0.0) if i == j else found

    c0, c1, c2 = (cross_ref[:, i * b : (i + 1) * b] for i in range(3))
    a01, a02, a12 = block(0, 1), block(0, 2), block(1, 2)
    a10, a20, a21 = block(1, 0), block(2, 0), block(2, 1)
    i0 = inverse(block(0, 0), PIVOTS)
    u01 = product(i0, a01)
    u02 = product(i0, a02)
    y0 = product(c0, i0)
    i1 = inverse(block(1, 1) - product(a10, u01), PIVOTS)
    a12 = a12 - product(a10, u02)
    a21 = a21 - product(a20, u01)
    a22 = block(2, 2) - product(a20, u02)
    z1 = c1 - product(y0, a01)
    z2 = c2 - product(y0, a02)
    between()
    u12 = product(i1, a12)
    y1 = product(z1, i1)
    i2 = inverse(a22 - product(a21, u12), PIVOTS)
    z2 = z2 - product(y1, a12)
    x2 = product(z2, i2)
    x1 = product(z1 - product(x2, a21), i1)
    x0 = product(c0 - product(x1, a10) - product(x2, a20), i0)
    return jnp.concatenate([x0, x1, x2], axis=1)


def on_device(log_modulus, basis, sensitivity, obs_block, observed, noise_scale, perturbation):
    n_obs = sensitivity.shape[0]
    return log_modulus + update(
        log_modulus, basis, sensitivity, obs_block.reshape(1, n_obs),
        observed.reshape(1, n_obs), noise_scale.reshape(1, n_obs), perturbation,
    )


def solution(mesh):
    in_specs = (
        P("grp", "vox"), P(), P("vox", None), P("vox", None), P("vox"), P("vox"), P("grp", "vox"),
    )
    return jax.shard_map(
        on_device, mesh=mesh, in_specs=in_specs, out_specs=P("grp", "vox"), check_vma=False
    )
```

```python
import functools
import math

import jax
import jax.numpy as jnp
from jax import lax
from jax.experimental import pallas as pl
from jax.experimental.pallas import tpu as pltpu
from jax.sharding import PartitionSpec as P

MESH = pl.DeviceIdType.MESH
HIGHEST = lax.Precision.HIGHEST
NX, NY, NZ, NC = 4, 8, 8, 2
N_VOX, N_GRP = NX * NY, NZ * NC
SIDE = 128
PIVOTS = 8
TILE = (8, 128)
PIECE = (16, 128)
QUAD = 4
CAP = 8
ROWS = 16


def remote(src, dst, send_sem, recv_sem, device):
    return pltpu.make_async_remote_copy(
        src_ref=src, dst_ref=dst, send_sem=send_sem, recv_sem=recv_sem,
        device_id=device, device_id_type=MESH,
    )


def update_kernel(
    lm_hbm, basis_hbm, sens_hbm, blk_ref, obs_ref, noise_ref, pert_hbm,
    out_ref,
    lm_ref, basis_ref, sens_ref, pert_ref, in_sem, abuf, gram_ref, cross_ref,
    xout, xin, pbuf, phi, pred_ref, part, rbuf, tot, gbuf, mbuf, msum,
    xs_sem, xr_sem, hs_sem, hr_sem, cs_sem, cr_sem, ds_sem, dr_sem, dps_sem, dpr_sem,
    rs_sem, rr_sem, as_sem, ar_sem, gs_sem, gr_sem, ms_sem, mr_sem, mps_sem, mpr_sem,
    fs_sem, fr_sem, fps_sem, fpr_sem,
):
    g = lax.axis_index("grp")
    v = lax.axis_index("vox")
    z, core = g // NC, g % NC
    x, y = v // NY, v % NY
    partner = z * NC + (1 - core)
    j_dev, vox_dev = lm_ref.shape
    block_vox, width = basis_ref.shape
    blocks_dev = vox_dev // block_vox
    n_obs = sens_ref.shape[0]
    members = j_dev * N_GRP
    scale_root = math.sqrt(members - 1)

    in_blocks = [slice(b * block_vox, (b + 1) * block_vox) for b in range(blocks_dev)]
    pairs = [(lm_hbm.at[:, cut], lm_ref.at[:, cut]) for cut in in_blocks]
    pairs += [(basis_hbm, basis_ref), (sens_hbm, sens_ref), (pert_hbm, pert_ref)]
    fetches = [pltpu.make_async_copy(src, dst, in_sem.at[i]) for i, (src, dst) in enumerate(pairs)]
    for fetch in fetches:
        fetch.start()
    barrier = pltpu.get_barrier_semaphore()

    def greet_vox(i, _):
        pl.semaphore_signal(barrier, inc=1, device_id={"vox": (v + i) % N_VOX}, device_id_type=MESH)
        return 0

    def z_peer(i):
        return ((z + i) % NZ) * NC + core

    def greet_grp(i, _):
        pl.semaphore_signal(barrier, inc=1, device_id={"grp": z_peer(i)}, device_id_type=MESH)
        return 0

    lax.fori_loop(1, N_VOX, greet_vox, 0)
    lax.fori_loop(1, NZ, greet_grp, 0)
    pl.semaphore_signal(barrier, inc=1, device_id={"grp": partner}, device_id_type=MESH)

    strips = []
    for b in range(blocks_dev):
        fetches[b].wait()
        strips.append(jnp.exp(-lm_ref[:, in_blocks[b]]))
    stacked = jnp.concatenate(strips, axis=0).astype(jnp.bfloat16)
    fetches[blocks_dev].wait()
    features = jnp.dot(stacked, basis_ref[...], preferred_element_type=jnp.float32)
    wide = jnp.concatenate([features[b * j_dev : (b + 1) * j_dev] for b in range(blocks_dev)], axis=1)
    f_half = blocks_dev * width // 2
    pbuf[g] = jnp.concatenate([wide[:, :f_half], wide[:, f_half:]], axis=0).astype(jnp.bfloat16)
    lane_half = vox_dev // 2
    pl.semaphore_wait(barrier, N_VOX - 1 + NZ - 1 + 1)

    def peer_copy(i, arriving):
        slot = pbuf.at[((z + NZ - i) % NZ) * NC + core if arriving else g]
        return remote(slot, slot, ds_sem.at[i], dr_sem.at[i], {"grp": z_peer(i)})

    def partner_copy(i, arriving):
        slot = pbuf.at[((z + NZ - i) % NZ) * NC + (1 - core if arriving else core)]
        return remote(slot, slot, dps_sem.at[i], dpr_sem.at[i], {"grp": partner})

    def send_peer(i, _):
        peer_copy(i, False).start()
        return 0

    def forward(i, _):
        peer_copy(i, True).wait_recv()
        partner_copy(i, False).start()
        return 0

    def from_partner(i, _):
        partner_copy(i, True).wait_recv()
        return 0

    lax.fori_loop(1, NZ, send_peer, 0)
    partner_copy(0, False).start()

    z_last = NZ // 2

    def field_part(slot, way, step):
        if step < z_last:
            return abuf.at[slot]
        return abuf.at[slot, :, pl.ds(way * (lane_half // 2), lane_half // 2)]

    def field_copy(way, step, arriving):
        turn = 1 if way == 0 else NZ - 1
        back = step if arriving else step - 1
        slot = ((z + (NZ - turn) * back) % NZ) * NC + core
        ref = field_part(slot, way, step)
        return remote(ref, ref, fs_sem.at[way, step - 1], fr_sem.at[way, step - 1],
                      {"grp": ((z + turn) % NZ) * NC + core})

    def field_partner(i, arriving):
        slot = ((z + NZ - i) % NZ) * NC + (1 - core if arriving else core)
        return remote(abuf.at[slot], abuf.at[slot], fps_sem.at[i], fpr_sem.at[i], {"grp": partner})

    def field_step(step):
        for way in range(2):
            if step > 0:
                field_copy(way, step, True).wait_recv()
            if step < z_last:
                field_copy(way, step + 1, False).start()
        if step in (0, z_last):
            field_partner(step, False).start()
        else:
            field_partner(step, False).start()
            field_partner(NZ - step, False).start()

    n_blocks = blocks_dev * N_VOX
    slots = blocks_dev * CAP
    groups = slots // ROWS
    blk = blk_ref[...]
    hit = (lax.broadcasted_iota(jnp.int32, (n_blocks, n_obs), 0) == blk).astype(jnp.float32)
    before = (
        lax.broadcasted_iota(jnp.int32, (n_obs, n_obs), 0)
        < lax.broadcasted_iota(jnp.int32, (n_obs, n_obs), 1)
    ).astype(jnp.float32)
    counts = jnp.dot(
        hit.astype(jnp.bfloat16), before.astype(jnp.bfloat16), preferred_element_type=jnp.float32
    )
    rank = jnp.sum(hit * counts, axis=0, keepdims=True)
    slot_of = blk * CAP + rank.astype(jnp.int32)

    def three(value):
        first = value.astype(jnp.bfloat16).astype(jnp.float32)
        second = (value - first).astype(jnp.bfloat16).astype(jnp.float32)
        return first, second, value - first - second

    observed = obs_ref[...]
    sub = lax.broadcasted_iota(jnp.int32, (8, n_obs), 0)
    tail = jnp.zeros((8, n_obs), jnp.float32)
    for i, term in enumerate((*three(observed), *three(1.0 / noise_ref[...]))):
        tail = jnp.where(sub == i, term, tail)
    fetches[blocks_dev + 1].wait()
    fetches[blocks_dev + 2].wait()
    with_obs = jnp.concatenate([pert_ref[...], tail], axis=0).astype(jnp.bfloat16)
    row_id = lax.broadcasted_iota(jnp.int32, (N_VOX * ROWS, n_obs), 0)
    code = row_id + (slots - ROWS) * lax.shift_right_logical(row_id, ROWS.bit_length() - 1)
    extras = []
    for q in range(groups):
        take = (code == slot_of - ROWS * q).astype(jnp.float32).astype(jnp.bfloat16)
        rows_q = jnp.dot(take, sens_ref[...], preferred_element_type=jnp.float32)
        xout[:, ROWS * q : ROWS * (q + 1), :] = rows_q.astype(jnp.bfloat16).reshape(N_VOX, ROWS, width)
        extras.append(
            lax.dot_general(take, with_obs, (((1,), (1,)), ((), ())), preferred_element_type=jnp.float32)
        )
    beside = jnp.concatenate(extras, axis=1).astype(jnp.bfloat16)
    xout[:, slots : slots + ROWS, :] = beside.reshape(N_VOX, ROWS, width)

    part_rows = slots // NC
    own_half = pl.ds(pl.multiple_of(core * part_rows, 16), part_rows)
    other_half = pl.ds(pl.multiple_of((1 - core) * part_rows, 16), part_rows)
    beside_rows = pl.ds(slots, ROWS)

    def half_copy(i):
        to = (v + i) % N_VOX
        return remote(xout.at[to, own_half], xin.at[v, own_half], hs_sem, hr_sem.at[i], {"vox": to})

    def half_from(i, which):
        slot = xin.at[(v + N_VOX - i) % N_VOX, which]
        return remote(slot, slot, cs_sem, cr_sem, {"grp": partner})

    def send_rows(i, _):
        to = (v + i) % N_VOX
        half_copy(i).start()
        remote(xout.at[to, beside_rows], xin.at[v, beside_rows], xs_sem, xr_sem, {"vox": to}).start()
        return 0

    def pass_half(i, _):
        slot = xin.at[(v + N_VOX - i) % N_VOX, own_half]
        remote(slot, slot, hs_sem, hr_sem.at[i], {"grp": partner}).wait_recv()
        half_from(i, own_half).start()
        return 0

    lax.fori_loop(1, N_VOX, send_rows, 0)
    xin[v] = xout[v]
    lm = lm_ref[...]
    abuf[g] = jnp.concatenate([lm[:, :lane_half], lm[:, lane_half:]], axis=0).astype(jnp.bfloat16)
    lax.fori_loop(1, NZ, forward, 0)
    lax.fori_loop(0, NZ, from_partner, 0)

    def features_of(group):
        d = pbuf[group].astype(jnp.float32)
        return jnp.concatenate([d[:j_dev], d[j_dev:]], axis=1)

    def place_pair(n, _):
        both = jnp.concatenate([features_of(2 * n), features_of(2 * n + 1)], axis=0)
        rows = 2 * j_dev
        phi[pl.ds(pl.multiple_of(n * rows, 16), rows), :] = both.astype(jnp.bfloat16)
        return 0

    lax.fori_loop(0, NZ, place_pair, 0)
    field_step(0)
    lax.fori_loop(1, N_VOX, pass_half, 0)
    got_beside = xin.at[pl.ds(0, N_VOX - 1), beside_rows]
    got_halves = xin.at[pl.ds(0, N_VOX - 1), pl.ds(0, part_rows)]
    pltpu.make_async_copy(got_beside, got_beside, xr_sem).wait()
    pltpu.make_async_copy(got_halves, got_halves, cr_sem).wait()

    n_here = N_VOX * ROWS
    extra = xin[:, slots : slots + ROWS, :].astype(jnp.float32).reshape(n_here, width).T
    per = width // groups
    low = (lax.broadcasted_iota(jnp.int32, (n_here, width), 0) & (ROWS - 1)) < CAP
    u = z % 2 * NC + core
    share = SIDE // QUAD
    n_side = members // SIDE
    sums = jnp.zeros((n_side * share + j_dev, members), jnp.float32)
    lanes = jnp.zeros(TILE, jnp.float32)
    pair = 2 * width
    contract = (((1,), (1,)), ((), ()))
    for q in range(groups):
        rows_q = xin[:, ROWS * q : ROWS * (q + 1), :].astype(jnp.float32).reshape(n_here, width)
        both = jnp.concatenate([jnp.where(low, rows_q, 0.0), jnp.where(low, 0.0, rows_q)], axis=1)
        pred = lax.dot_general(
            phi[:, pair * q : pair * (q + 1)], both.astype(jnp.bfloat16), contract,
            preferred_element_type=jnp.float32,
        )
        pred_ref[...] = pred
        centre = jnp.sum(pred, axis=0, keepdims=True) * (1.0 / members)
        at = per * q + j_dev
        seen = extra[at : at + 1] + extra[at + 1 : at + 2] + extra[at + 2 : at + 3]
        inv_noise = extra[at + 3 : at + 4] + extra[at + 4 : at + 5] + extra[at + 5 : at + 6]
        scale = inv_noise * (1.0 / scale_root)
        scaled = ((pred - centre) * scale).astype(jnp.bfloat16)
        own_pred = pred_ref[pl.ds(pl.multiple_of(g * j_dev, 8), j_dev), :]
        misfit = (seen - own_pred) * inv_noise + extra[per * q : per * q + j_dev]
        misfit = misfit.astype(jnp.bfloat16).astype(jnp.float32)
        some = [
            pred_ref[pl.ds(pl.multiple_of(side * SIDE + u * share, 8), share), :] for side in range(n_side)
        ]
        left = jnp.concatenate([(p - centre) * scale for p in some] + [misfit], axis=0)
        left = left.astype(jnp.bfloat16)
        sums = sums + lax.dot_general(left, scaled, contract, preferred_element_type=jnp.float32)
        squares = misfit * misfit
        for i in range(j_dev // 8):
            for c in range(n_here // 128):
                lanes = lanes + squares[8 * i : 8 * i + 8, 128 * c : 128 * c + 128]

    n_row, n_col = j_dev // 8, members // 128
    strips_u = share // 8
    gram_at = [(side, strip, (side + turn) % n_side)
               for side in range(n_side) for strip in range(strips_u) for turn in range(2)]
    tiles = [sums[side * share + 8 * strip : side * share + 8 * strip + 8, SIDE * k : SIDE * (k + 1)]
             for side, strip, k in gram_at]
    n_gram = len(tiles)
    n_pieces = n_gram // 2
    tiles.append(lanes)
    first_cross = n_side * share
    for i in range(n_row):
        for c in range(n_col):
            tiles.append(sums[first_cross + 8 * i : first_cross + 8 * i + 8, 128 * c : 128 * c + 128])
    for t, tile in enumerate(tiles):
        part[t // 2, t % 2 * 8 : t % 2 * 8 + 8] = tile
    n_tiles = len(tiles) // 2

    def send_part(i, _):
        t = (v + i) % n_tiles

        @pl.when(t != v)
        def _():
            remote(part.at[t], rbuf.at[v], rs_sem, rr_sem, {"vox": t}).start()

        return 0

    lax.fori_loop(0, n_tiles, send_part, 0)
    field_step(1)

    @pl.when(v < n_tiles)
    def _():
        rbuf[v] = part[v]
        got = rbuf.at[pl.ds(0, N_VOX - 1)]
        pltpu.make_async_copy(got, got, rr_sem).wait()
        tot[v] = jnp.sum(rbuf[...], axis=0)

        def spread(i, _):
            remote(tot.at[v], tot.at[v], as_sem, ar_sem, {"vox": (v + i) % N_VOX}).start()
            return 0

        lax.fori_loop(1, N_VOX, spread, 0)
        most = tot.at[pl.ds(0, n_tiles - 1)]
        pltpu.make_async_copy(most, most, ar_sem).wait()

    @pl.when(v >= n_tiles)
    def _():
        whole = tot.at[pl.ds(0, n_tiles)]
        pltpu.make_async_copy(whole, whole, ar_sem).wait()

    gbuf[u] = tot[0:n_pieces]
    mbuf[z] = tot[n_pieces, 0:8]
    beyond = {"grp": (z + 1 - z % 2 * 2) * NC + core}
    u_beyond = (1 - z % 2) * NC + core

    def gram_copy(n, slot, to):
        return remote(gbuf.at[slot], gbuf.at[slot], gs_sem.at[n], gr_sem.at[n], to)

    def squares_copy(i, arriving):
        slot = mbuf.at[(z + NZ - i) % NZ if arriving else z]
        return remote(slot, slot, ms_sem.at[i], mr_sem.at[i], {"grp": z_peer(i)})

    gram_copy(0, u, beyond).start()
    gram_copy(1, u, {"grp": partner}).start()

    def squares_send(i, _):
        squares_copy(i, False).start()
        return 0

    lax.fori_loop(1, NZ, squares_send, 0)
    field_step(2)
    for i in range(n_row):
        for c in range(n_col):
            t = n_gram + 1 + i * n_col + c
            cross_ref[8 * i : 8 * i + 8, 128 * c : 128 * c + 128] = tot[t // 2, t % 2 * 8 : t % 2 * 8 + 8]
    gram_copy(0, u_beyond, beyond).wait_recv()
    gram_copy(2, u_beyond, {"grp": partner}).start()

    def squares_wait(i, _):
        squares_copy(i, True).wait_recv()
        return 0

    lax.fori_loop(1, NZ, squares_wait, 0)
    msum[core] = jnp.sum(mbuf[...], axis=0)
    squares_across = remote(msum.at[core], msum.at[core], mps_sem, mpr_sem, {"grp": partner})
    squares_across.start()
    gram_copy(1, z % 2 * NC + 1 - core, {"grp": partner}).wait_recv()
    gram_copy(2, (1 - z % 2) * NC + 1 - core, {"grp": partner}).wait_recv()
    for n in range(QUAD):
        for t, (side, strip, k) in enumerate(gram_at):
            row = side * SIDE + n * share + 8 * strip
            gram_ref[row : row + 8, SIDE * k : SIDE * (k + 1)] = gbuf[n, t // 2, t % 2 * 8 : t % 2 * 8 + 8]
    remote(msum.at[1 - core], msum.at[1 - core], mps_sem, mpr_sem, {"grp": partner}).wait_recv()
    damping = jnp.sum(msum[0] + msum[1], keepdims=True) * (1.0 / (members * n_obs * N_VOX))
    weights = solve(gram_ref, cross_ref, damping, field_step).astype(jnp.bfloat16)

    def field_from(i, _):
        field_partner(i, True).wait_recv()
        return 0

    lax.fori_loop(0, NZ, field_from, 0)
    col = lax.broadcasted_iota(jnp.int32, (members, 2 * members), 1)
    row = lax.broadcasted_iota(jnp.int32, (members, 2 * members), 0)
    group = jnp.floor((row.astype(jnp.float32) + 0.5) * (1.0 / j_dev)).astype(jnp.int32)
    place_of = row + group * j_dev
    spread_weights = jnp.concatenate(
        [
            jnp.dot(weights, (col == place_of + j_dev * h).astype(jnp.bfloat16),
                    preferred_element_type=jnp.float32)
            for h in range(2)
        ],
        axis=0,
    ).astype(jnp.bfloat16)
    piece = 512
    for n in range(lane_half // piece):
        cut = slice(n * piece, (n + 1) * piece)
        field = abuf[:, :, cut].reshape(2 * members, piece)
        mixture = jnp.dot(spread_weights, field, preferred_element_type=jnp.float32) * (1.0 / scale_root)
        for h in range(2):
            cols = slice(h * lane_half + n * piece, h * lane_half + (n + 1) * piece)
            out_ref[:, cols] = mixture[h * j_dev : (h + 1) * j_dev]

    pltpu.make_async_copy(got_beside, got_beside, xs_sem).wait()
    pltpu.make_async_copy(got_halves, got_halves, hs_sem).wait()
    pltpu.make_async_copy(got_halves, got_halves, cs_sem).wait()
    def grp_sent(i, _):
        peer_copy(i, False).wait_send()
        squares_copy(i, False).wait_send()
        return 0

    def partner_sent(i, _):
        for copy in (partner_copy(i, False), field_partner(i, False)):
            copy.wait_send()
        return 0

    lax.fori_loop(1, NZ, grp_sent, 0)
    lax.fori_loop(0, NZ, partner_sent, 0)
    for n in range(3):
        gram_copy(n, u, {"grp": partner}).wait_send()
    squares_across.wait_send()
    for way in range(2):
        for step in range(1, z_last + 1):
            field_copy(way, step, False).wait_send()

    @pl.when(v < n_tiles)
    def _():
        sent = part.at[pl.ds(0, n_tiles - 1)]
        pltpu.make_async_copy(sent, sent, rs_sem).wait()
        spread_all = rbuf.at[pl.ds(0, N_VOX - 1)]
        pltpu.make_async_copy(spread_all, spread_all, as_sem).wait()

    @pl.when(v >= n_tiles)
    def _():
        sent = part.at[pl.ds(0, n_tiles)]
        pltpu.make_async_copy(sent, sent, rs_sem).wait()


def update(log_modulus, basis, sensitivity, blocks, observed, noise, perturbation):
    j_dev, vox_dev = log_modulus.shape
    block_vox, width = basis.shape
    blocks_dev = vox_dev // block_vox
    n_obs = sensitivity.shape[0]
    members = j_dev * N_GRP
    n_gram = (members // SIDE) * (SIDE // QUAD // 8) * 2
    n_tiles = (n_gram + 1 + (j_dev // 8) * (members // 128)) // 2
    f32, bf16 = jnp.float32, jnp.bfloat16
    dma = pltpu.SemaphoreType.DMA
    vmem = pl.BlockSpec(memory_space=pltpu.VMEM)
    hbm = pl.BlockSpec(memory_space=pltpu.HBM)
    return pl.pallas_call(
        update_kernel,
        out_shape=jax.ShapeDtypeStruct((j_dev, vox_dev), f32),
        in_specs=[hbm, hbm, hbm, vmem, vmem, vmem, hbm],
        out_specs=vmem,
        scratch_shapes=[
            pltpu.VMEM((j_dev, vox_dev), f32),
            pltpu.VMEM((block_vox, width), bf16),
            pltpu.VMEM((n_obs, width), bf16),
            pltpu.VMEM((j_dev, n_obs), f32),
            dma((blocks_dev + 3,)),
            pltpu.VMEM((N_GRP, 2 * j_dev, vox_dev // 2), bf16),
            pltpu.VMEM((members, members), f32),
            pltpu.VMEM((j_dev, members), f32),
            pltpu.VMEM((N_VOX, blocks_dev * CAP + ROWS, width), bf16),
            pltpu.VMEM((N_VOX, blocks_dev * CAP + ROWS, width), bf16),
            pltpu.VMEM((N_GRP, 2 * j_dev, blocks_dev * width // 2), bf16),
            pltpu.VMEM((members, blocks_dev * width), bf16),
            pltpu.VMEM((members, N_VOX * ROWS), f32),
            pltpu.VMEM((n_tiles, *PIECE), f32),
            pltpu.VMEM((N_VOX, *PIECE), f32),
            pltpu.VMEM((n_tiles, *PIECE), f32),
            pltpu.VMEM((QUAD, n_gram // 2, *PIECE), f32),
            pltpu.VMEM((NZ, *TILE), f32),
            pltpu.VMEM((NC, *TILE), f32),
            dma, dma, dma, dma((N_VOX,)), dma, dma, dma((NZ,)), dma((NZ,)), dma((NZ,)), dma((NZ,)),
            dma, dma, dma, dma,
            dma((3,)), dma((3,)), dma((NZ,)), dma((NZ,)), dma, dma,
            dma((2, NZ // 2)), dma((2, NZ // 2)), dma((NZ,)), dma((NZ,)),
        ],
        compiler_params=pltpu.CompilerParams(
            collective_id=0, has_side_effects=True, vmem_limit_bytes=62 << 20
        ),
        name="update",
    )(log_modulus, basis, sensitivity, blocks, observed, noise, perturbation)


def product(a, b):
    return lax.dot_general(
        a, b, (((1,), (0,)), ((), ())), precision=HIGHEST, preferred_element_type=jnp.float32
    )


def inverse(d, k):
    n = d.shape[0]
    lane = lax.broadcasted_iota(jnp.int32, (1, n), 1)
    sub = lax.broadcasted_iota(jnp.int32, (n, 1), 0)
    for p in range(0, n, k):
        cols = [jnp.broadcast_to(d[:, p + j : p + j + 1], (n, n)) for j in range(k)]
        s = [[cols[j][p + i : p + i + 1] for j in range(k)] for i in range(k)]
        inside = (lane >= p) & (lane < p + k)
        rows = [
            jnp.where(inside, (lane == p + i).astype(jnp.float32), d[p + i : p + i + 1])
            for i in range(k)
        ]
        for i in range(k):
            inv = 1.0 / s[i][i]
            rows[i] = rows[i] * inv
            for j in range(i + 1, k):
                s[i][j] = s[i][j] * inv
            for r in range(k):
                if r != i:
                    rows[r] = rows[r] - s[r][i] * rows[i]
                    for j in range(i + 1, k):
                        s[r][j] = s[r][j] - s[r][i] * s[i][j]
        row_in = (sub >= p) & (sub < p + k)
        d = jnp.where(inside | row_in, 0.0, d)
        for j in range(k):
            d = d - jnp.where(row_in, jnp.where(sub == p + j, -1.0, 0.0), cols[j]) * rows[j]
    return d


def solve(gram_ref, cross_ref, damp, between):
    b = SIDE
    eye = lax.broadcasted_iota(jnp.int32, (b, b), 0) == lax.broadcasted_iota(jnp.int32, (b, b), 1)

    def block(i, j):
        found = gram_ref[i * b : (i + 1) * b, j * b : (j + 1) * b]
        return found + jnp.where(eye, damp, 0.0) if i == j else found

    c0, c1, c2 = (cross_ref[:, i * b : (i + 1) * b] for i in range(3))
    a01, a12, a20 = block(0, 1), block(1, 2), block(2, 0)
    a10, a02 = a01.T, a20.T
    i0 = inverse(block(0, 0), PIVOTS)
    between(3)
    u01 = product(i0, a01)
    u02 = product(i0, a02)
    y0 = product(c0, i0)
    i1 = inverse(block(1, 1) - product(a10, u01), PIVOTS)
    a12 = a12 - product(a10, u02)
    a21 = a12.T
    a22 = block(2, 2) - product(a20, u02)
    z1 = c1 - product(y0, a01)
    z2 = c2 - product(y0, a02)
    u12 = product(i1, a12)
    y1 = product(z1, i1)
    i2 = inverse(a22 - product(a21, u12), PIVOTS)
    between(NZ // 2)
    z2 = z2 - product(y1, a12)
    x2 = product(z2, i2)
    x1 = product(z1 - product(x2, a21), i1)
    x0 = product(c0 - product(x1, a10) - product(x2, a20), i0)
    return jnp.concatenate([x0, x1, x2], axis=1)


def on_device(log_modulus, basis, sensitivity, obs_block, observed, noise_scale, perturbation):
    n_obs = sensitivity.shape[0]
    return log_modulus + update(
        log_modulus, basis, sensitivity, obs_block.reshape(1, n_obs),
        observed.reshape(1, n_obs), noise_scale.reshape(1, n_obs), perturbation,
    )


def solution(mesh):
    in_specs = (
        P("grp", "vox"), P(), P("vox", None), P("vox", None), P("vox"), P("vox"), P("grp", "vox"),
    )
    return jax.shard_map(
        on_device, mesh=mesh, in_specs=in_specs, out_specs=P("grp", "vox"), check_vma=False
    )
```

```python
import functools
import math

import jax
import jax.numpy as jnp
from jax import lax
from jax.experimental import pallas as pl
from jax.experimental.pallas import tpu as pltpu
from jax.sharding import PartitionSpec as P

MESH = pl.DeviceIdType.MESH
HIGHEST = lax.Precision.HIGHEST
NX, NY, NZ, NC = 4, 8, 8, 2
N_VOX, N_GRP = NX * NY, NZ * NC
SIDE = 128
PIVOTS = 8
TILE = (8, 128)
PIECE = (16, 128)
QUAD = 4
CAP = 8
ROWS = 16


def remote(src, dst, send_sem, recv_sem, device):
    return pltpu.make_async_remote_copy(
        src_ref=src, dst_ref=dst, send_sem=send_sem, recv_sem=recv_sem,
        device_id=device, device_id_type=MESH,
    )


def update_kernel(
    lm_hbm, basis_hbm, sens_hbm, blk_ref, obs_ref, noise_ref, pert_hbm,
    out_ref,
    lm_ref, basis_ref, sens_ref, pert_ref, in_sem, abuf, gram_ref, cross_ref,
    xout, xin, pbuf, phi, pred_ref, part, rbuf, tot, gbuf, mbuf, msum,
    xs_sem, xr_sem, hs_sem, hr_sem, cs_sem, cr_sem, ds_sem, dr_sem, dps_sem, dpr_sem,
    rs_sem, rr_sem, as_sem, ar_sem, gs_sem, gr_sem, ms_sem, mr_sem, mps_sem, mpr_sem,
    fs_sem, fr_sem, fps_sem, fpr_sem,
):
    g = lax.axis_index("grp")
    v = lax.axis_index("vox")
    z, core = g // NC, g % NC
    x, y = v // NY, v % NY
    partner = z * NC + (1 - core)
    j_dev, vox_dev = lm_ref.shape
    block_vox, width = basis_ref.shape
    blocks_dev = vox_dev // block_vox
    n_obs = sens_ref.shape[0]
    members = j_dev * N_GRP
    scale_root = math.sqrt(members - 1)

    in_blocks = [slice(b * block_vox, (b + 1) * block_vox) for b in range(blocks_dev)]
    pairs = [(lm_hbm.at[:, cut], lm_ref.at[:, cut]) for cut in in_blocks]
    pairs += [(basis_hbm, basis_ref), (sens_hbm, sens_ref), (pert_hbm, pert_ref)]
    fetches = [pltpu.make_async_copy(src, dst, in_sem.at[i]) for i, (src, dst) in enumerate(pairs)]
    for fetch in fetches:
        fetch.start()
    barrier = pltpu.get_barrier_semaphore()

    def greet_vox(i, _):
        pl.semaphore_signal(barrier, inc=1, device_id={"vox": (v + i) % N_VOX}, device_id_type=MESH)
        return 0

    def z_peer(i):
        return ((z + i) % NZ) * NC + core

    def greet_grp(i, _):
        pl.semaphore_signal(barrier, inc=1, device_id={"grp": z_peer(i)}, device_id_type=MESH)
        return 0

    lax.fori_loop(1, N_VOX, greet_vox, 0)
    lax.fori_loop(1, NZ, greet_grp, 0)
    pl.semaphore_signal(barrier, inc=1, device_id={"grp": partner}, device_id_type=MESH)

    strips = []
    for b in range(blocks_dev):
        fetches[b].wait()
        strips.append(jnp.exp(-lm_ref[:, in_blocks[b]]))
    stacked = jnp.concatenate(strips, axis=0).astype(jnp.bfloat16)
    fetches[blocks_dev].wait()
    features = jnp.dot(stacked, basis_ref[...], preferred_element_type=jnp.float32)
    wide = jnp.concatenate([features[b * j_dev : (b + 1) * j_dev] for b in range(blocks_dev)], axis=1)
    f_half = blocks_dev * width // 2
    pbuf[g] = jnp.concatenate([wide[:, :f_half], wide[:, f_half:]], axis=0).astype(jnp.bfloat16)
    lane_half = vox_dev // 2
    pl.semaphore_wait(barrier, N_VOX - 1 + NZ - 1 + 1)

    def peer_copy(i, arriving):
        slot = pbuf.at[((z + NZ - i) % NZ) * NC + core if arriving else g]
        return remote(slot, slot, ds_sem.at[i], dr_sem.at[i], {"grp": z_peer(i)})

    def partner_copy(i, arriving):
        slot = pbuf.at[((z + NZ - i) % NZ) * NC + (1 - core if arriving else core)]
        return remote(slot, slot, dps_sem.at[i], dpr_sem.at[i], {"grp": partner})

    def send_peer(i, _):
        peer_copy(i, False).start()
        return 0

    def forward(i, _):
        peer_copy(i, True).wait_recv()
        partner_copy(i, False).start()
        return 0

    def from_partner(i, _):
        partner_copy(i, True).wait_recv()
        return 0

    lax.fori_loop(1, NZ, send_peer, 0)
    partner_copy(0, False).start()

    z_last = NZ // 2

    def field_part(slot, way, step):
        if step < z_last:
            return abuf.at[slot]
        return abuf.at[slot, :, pl.ds(way * (lane_half // 2), lane_half // 2)]

    def field_copy(way, step, arriving):
        turn = 1 if way == 0 else NZ - 1
        back = step if arriving else step - 1
        slot = ((z + (NZ - turn) * back) % NZ) * NC + core
        ref = field_part(slot, way, step)
        return remote(ref, ref, fs_sem.at[way, step - 1], fr_sem.at[way, step - 1],
                      {"grp": ((z + turn) % NZ) * NC + core})

    def field_partner(i, arriving):
        slot = ((z + NZ - i) % NZ) * NC + (1 - core if arriving else core)
        return remote(abuf.at[slot], abuf.at[slot], fps_sem.at[i], fpr_sem.at[i], {"grp": partner})

    def field_step(step):
        for way in range(2):
            if step > 0:
                field_copy(way, step, True).wait_recv()
            if step < z_last:
                field_copy(way, step + 1, False).start()
        if step in (0, z_last):
            field_partner(step, False).start()
        else:
            field_partner(step, False).start()
            field_partner(NZ - step, False).start()

    n_blocks = blocks_dev * N_VOX
    slots = blocks_dev * CAP
    groups = slots // ROWS
    blk = blk_ref[...]
    hit = (lax.broadcasted_iota(jnp.int32, (n_blocks, n_obs), 0) == blk).astype(jnp.float32)
    before = (
        lax.broadcasted_iota(jnp.int32, (n_obs, n_obs), 0)
        < lax.broadcasted_iota(jnp.int32, (n_obs, n_obs), 1)
    ).astype(jnp.float32)
    counts = jnp.dot(
        hit.astype(jnp.bfloat16), before.astype(jnp.bfloat16), preferred_element_type=jnp.float32
    )
    rank = jnp.sum(hit * counts, axis=0, keepdims=True)
    slot_of = blk * CAP + rank.astype(jnp.int32)

    def three(value):
        first = value.astype(jnp.bfloat16).astype(jnp.float32)
        second = (value - first).astype(jnp.bfloat16).astype(jnp.float32)
        return first, second, value - first - second

    observed = obs_ref[...]
    sub = lax.broadcasted_iota(jnp.int32, (8, n_obs), 0)
    tail = jnp.zeros((8, n_obs), jnp.float32)
    for i, term in enumerate((*three(observed), *three(1.0 / noise_ref[...]))):
        tail = jnp.where(sub == i, term, tail)
    fetches[blocks_dev + 1].wait()
    fetches[blocks_dev + 2].wait()
    with_obs = jnp.concatenate([pert_ref[...], tail], axis=0).astype(jnp.bfloat16)
    row_id = lax.broadcasted_iota(jnp.int32, (N_VOX * ROWS, n_obs), 0)
    code = row_id + (slots - ROWS) * lax.shift_right_logical(row_id, ROWS.bit_length() - 1)
    extras = []
    for q in range(groups):
        take = (code == slot_of - ROWS * q).astype(jnp.float32).astype(jnp.bfloat16)
        rows_q = jnp.dot(take, sens_ref[...], preferred_element_type=jnp.float32)
        xout[:, ROWS * q : ROWS * (q + 1), :] = rows_q.astype(jnp.bfloat16).reshape(N_VOX, ROWS, width)
        extras.append(
            lax.dot_general(take, with_obs, (((1,), (1,)), ((), ())), preferred_element_type=jnp.float32)
        )
    beside = jnp.concatenate(extras, axis=1).astype(jnp.bfloat16)
    xout[:, slots : slots + ROWS, :] = beside.reshape(N_VOX, ROWS, width)

    part_rows = slots // NC
    own_half = pl.ds(pl.multiple_of(core * part_rows, 16), part_rows)
    other_half = pl.ds(pl.multiple_of((1 - core) * part_rows, 16), part_rows)
    beside_rows = pl.ds(slots, ROWS)

    def half_copy(i):
        to = (v + i) % N_VOX
        return remote(xout.at[to, own_half], xin.at[v, own_half], hs_sem, hr_sem.at[i], {"vox": to})

    def half_from(i, which):
        slot = xin.at[(v + N_VOX - i) % N_VOX, which]
        return remote(slot, slot, cs_sem, cr_sem, {"grp": partner})

    def send_rows(i, _):
        to = (v + i) % N_VOX
        half_copy(i).start()
        remote(xout.at[to, beside_rows], xin.at[v, beside_rows], xs_sem, xr_sem, {"vox": to}).start()
        return 0

    def pass_half(i, _):
        slot = xin.at[(v + N_VOX - i) % N_VOX, own_half]
        remote(slot, slot, hs_sem, hr_sem.at[i], {"grp": partner}).wait_recv()
        half_from(i, own_half).start()
        return 0

    lax.fori_loop(1, N_VOX, send_rows, 0)
    xin[v] = xout[v]
    lm = lm_ref[...]
    abuf[g] = jnp.concatenate([lm[:, :lane_half], lm[:, lane_half:]], axis=0).astype(jnp.bfloat16)
    field_step(0)
    lax.fori_loop(1, NZ, forward, 0)
    lax.fori_loop(0, NZ, from_partner, 0)

    def features_of(group):
        d = pbuf[group].astype(jnp.float32)
        return jnp.concatenate([d[:j_dev], d[j_dev:]], axis=1)

    def place_pair(n, _):
        both = jnp.concatenate([features_of(2 * n), features_of(2 * n + 1)], axis=0)
        rows = 2 * j_dev
        phi[pl.ds(pl.multiple_of(n * rows, 16), rows), :] = both.astype(jnp.bfloat16)
        return 0

    lax.fori_loop(0, NZ, place_pair, 0)
    lax.fori_loop(1, N_VOX, pass_half, 0)
    field_step(1)
    got_beside = xin.at[pl.ds(0, N_VOX - 1), beside_rows]
    got_halves = xin.at[pl.ds(0, N_VOX - 1), pl.ds(0, part_rows)]
    pltpu.make_async_copy(got_beside, got_beside, xr_sem).wait()
    pltpu.make_async_copy(got_halves, got_halves, cr_sem).wait()

    n_here = N_VOX * ROWS
    extra = xin[:, slots : slots + ROWS, :].astype(jnp.float32).reshape(n_here, width).T
    per = width // groups
    low = (lax.broadcasted_iota(jnp.int32, (n_here, width), 0) & (ROWS - 1)) < CAP
    u = z % 2 * NC + core
    share = SIDE // QUAD
    n_side = members // SIDE
    sums = jnp.zeros((n_side * share + j_dev, members), jnp.float32)
    lanes = jnp.zeros(TILE, jnp.float32)
    pair = 2 * width
    contract = (((1,), (1,)), ((), ()))
    for q in range(groups):
        rows_q = xin[:, ROWS * q : ROWS * (q + 1), :].astype(jnp.float32).reshape(n_here, width)
        both = jnp.concatenate([jnp.where(low, rows_q, 0.0), jnp.where(low, 0.0, rows_q)], axis=1)
        pred = lax.dot_general(
            phi[:, pair * q : pair * (q + 1)], both.astype(jnp.bfloat16), contract,
            preferred_element_type=jnp.float32,
        )
        pred_ref[...] = pred
        centre = jnp.sum(pred, axis=0, keepdims=True) * (1.0 / members)
        at = per * q + j_dev
        seen = extra[at : at + 1] + extra[at + 1 : at + 2] + extra[at + 2 : at + 3]
        inv_noise = extra[at + 3 : at + 4] + extra[at + 4 : at + 5] + extra[at + 5 : at + 6]
        scale = inv_noise * (1.0 / scale_root)
        scaled = ((pred - centre) * scale).astype(jnp.bfloat16)
        own_pred = pred_ref[pl.ds(pl.multiple_of(g * j_dev, 8), j_dev), :]
        misfit = (seen - own_pred) * inv_noise + extra[per * q : per * q + j_dev]
        misfit = misfit.astype(jnp.bfloat16).astype(jnp.float32)
        some = [
            pred_ref[pl.ds(pl.multiple_of(side * SIDE + u * share, 8), share), :] for side in range(n_side)
        ]
        left = jnp.concatenate([(p - centre) * scale for p in some] + [misfit], axis=0)
        left = left.astype(jnp.bfloat16)
        sums = sums + lax.dot_general(left, scaled, contract, preferred_element_type=jnp.float32)
        squares = misfit * misfit
        for i in range(j_dev // 8):
            for c in range(n_here // 128):
                lanes = lanes + squares[8 * i : 8 * i + 8, 128 * c : 128 * c + 128]

    n_row, n_col = j_dev // 8, members // 128
    strips_u = share // 8
    gram_at = [(side, strip, (side + turn) % n_side)
               for side in range(n_side) for strip in range(strips_u) for turn in range(2)]
    tiles = [sums[side * share + 8 * strip : side * share + 8 * strip + 8, SIDE * k : SIDE * (k + 1)]
             for side, strip, k in gram_at]
    n_gram = len(tiles)
    n_pieces = n_gram // 2
    tiles.append(lanes)
    first_cross = n_side * share
    for i in range(n_row):
        for c in range(n_col):
            tiles.append(sums[first_cross + 8 * i : first_cross + 8 * i + 8, 128 * c : 128 * c + 128])
    for t, tile in enumerate(tiles):
        part[t // 2, t % 2 * 8 : t % 2 * 8 + 8] = tile
    n_tiles = len(tiles) // 2

    def send_part(i, _):
        t = (v + i) % n_tiles

        @pl.when(t != v)
        def _():
            remote(part.at[t], rbuf.at[v], rs_sem, rr_sem, {"vox": t}).start()

        return 0

    lax.fori_loop(0, n_tiles, send_part, 0)
    field_step(2)

    @pl.when(v < n_tiles)
    def _():
        rbuf[v] = part[v]
        got = rbuf.at[pl.ds(0, N_VOX - 1)]
        pltpu.make_async_copy(got, got, rr_sem).wait()
        tot[v] = jnp.sum(rbuf[...], axis=0)

        def spread(i, _):
            remote(tot.at[v], tot.at[v], as_sem, ar_sem, {"vox": (v + i) % N_VOX}).start()
            return 0

        lax.fori_loop(1, N_VOX, spread, 0)
        most = tot.at[pl.ds(0, n_tiles - 1)]
        pltpu.make_async_copy(most, most, ar_sem).wait()

    @pl.when(v >= n_tiles)
    def _():
        whole = tot.at[pl.ds(0, n_tiles)]
        pltpu.make_async_copy(whole, whole, ar_sem).wait()

    gbuf[u] = tot[0:n_pieces]
    mbuf[z] = tot[n_pieces, 0:8]
    beyond = {"grp": (z + 1 - z % 2 * 2) * NC + core}
    u_beyond = (1 - z % 2) * NC + core

    def gram_copy(n, slot, to):
        return remote(gbuf.at[slot], gbuf.at[slot], gs_sem.at[n], gr_sem.at[n], to)

    def squares_copy(i, arriving):
        slot = mbuf.at[(z + NZ - i) % NZ if arriving else z]
        return remote(slot, slot, ms_sem.at[i], mr_sem.at[i], {"grp": z_peer(i)})

    gram_copy(0, u, beyond).start()
    gram_copy(1, u, {"grp": partner}).start()

    def squares_send(i, _):
        squares_copy(i, False).start()
        return 0

    lax.fori_loop(1, NZ, squares_send, 0)
    for i in range(n_row):
        for c in range(n_col):
            t = n_gram + 1 + i * n_col + c
            cross_ref[8 * i : 8 * i + 8, 128 * c : 128 * c + 128] = tot[t // 2, t % 2 * 8 : t % 2 * 8 + 8]
    gram_copy(0, u_beyond, beyond).wait_recv()
    gram_copy(2, u_beyond, {"grp": partner}).start()

    def squares_wait(i, _):
        squares_copy(i, True).wait_recv()
        return 0

    lax.fori_loop(1, NZ, squares_wait, 0)
    msum[core] = jnp.sum(mbuf[...], axis=0)
    squares_across = remote(msum.at[core], msum.at[core], mps_sem, mpr_sem, {"grp": partner})
    squares_across.start()
    gram_copy(1, z % 2 * NC + 1 - core, {"grp": partner}).wait_recv()
    gram_copy(2, (1 - z % 2) * NC + 1 - core, {"grp": partner}).wait_recv()
    for n in range(QUAD):
        for t, (side, strip, k) in enumerate(gram_at):
            row = side * SIDE + n * share + 8 * strip
            gram_ref[row : row + 8, SIDE * k : SIDE * (k + 1)] = gbuf[n, t // 2, t % 2 * 8 : t % 2 * 8 + 8]
    remote(msum.at[1 - core], msum.at[1 - core], mps_sem, mpr_sem, {"grp": partner}).wait_recv()
    damping = jnp.sum(msum[0] + msum[1], keepdims=True) * (1.0 / (members * n_obs * N_VOX))
    field_step(3)
    weights = solve(gram_ref, cross_ref, damping, field_step).astype(jnp.bfloat16)

    def field_from(i, _):
        field_partner(i, True).wait_recv()
        return 0

    lax.fori_loop(0, NZ, field_from, 0)
    col = lax.broadcasted_iota(jnp.int32, (members, 2 * members), 1)
    row = lax.broadcasted_iota(jnp.int32, (members, 2 * members), 0)
    group = jnp.floor((row.astype(jnp.float32) + 0.5) * (1.0 / j_dev)).astype(jnp.int32)
    place_of = row + group * j_dev
    spread_weights = jnp.concatenate(
        [
            jnp.dot(weights, (col == place_of + j_dev * h).astype(jnp.bfloat16),
                    preferred_element_type=jnp.float32)
            for h in range(2)
        ],
        axis=0,
    ).astype(jnp.bfloat16)
    piece = 512
    for n in range(lane_half // piece):
        cut = slice(n * piece, (n + 1) * piece)
        field = abuf[:, :, cut].reshape(2 * members, piece)
        mixture = jnp.dot(spread_weights, field, preferred_element_type=jnp.float32) * (1.0 / scale_root)
        for h in range(2):
            cols = slice(h * lane_half + n * piece, h * lane_half + (n + 1) * piece)
            out_ref[:, cols] = mixture[h * j_dev : (h + 1) * j_dev]

    pltpu.make_async_copy(got_beside, got_beside, xs_sem).wait()
    pltpu.make_async_copy(got_halves, got_halves, hs_sem).wait()
    pltpu.make_async_copy(got_halves, got_halves, cs_sem).wait()
    def grp_sent(i, _):
        peer_copy(i, False).wait_send()
        squares_copy(i, False).wait_send()
        return 0

    def partner_sent(i, _):
        for copy in (partner_copy(i, False), field_partner(i, False)):
            copy.wait_send()
        return 0

    lax.fori_loop(1, NZ, grp_sent, 0)
    lax.fori_loop(0, NZ, partner_sent, 0)
    for n in range(3):
        gram_copy(n, u, {"grp": partner}).wait_send()
    squares_across.wait_send()
    for way in range(2):
        for step in range(1, z_last + 1):
            field_copy(way, step, False).wait_send()

    @pl.when(v < n_tiles)
    def _():
        sent = part.at[pl.ds(0, n_tiles - 1)]
        pltpu.make_async_copy(sent, sent, rs_sem).wait()
        spread_all = rbuf.at[pl.ds(0, N_VOX - 1)]
        pltpu.make_async_copy(spread_all, spread_all, as_sem).wait()

    @pl.when(v >= n_tiles)
    def _():
        sent = part.at[pl.ds(0, n_tiles)]
        pltpu.make_async_copy(sent, sent, rs_sem).wait()


def update(log_modulus, basis, sensitivity, blocks, observed, noise, perturbation):
    j_dev, vox_dev = log_modulus.shape
    block_vox, width = basis.shape
    blocks_dev = vox_dev // block_vox
    n_obs = sensitivity.shape[0]
    members = j_dev * N_GRP
    n_gram = (members // SIDE) * (SIDE // QUAD // 8) * 2
    n_tiles = (n_gram + 1 + (j_dev // 8) * (members // 128)) // 2
    f32, bf16 = jnp.float32, jnp.bfloat16
    dma = pltpu.SemaphoreType.DMA
    vmem = pl.BlockSpec(memory_space=pltpu.VMEM)
    hbm = pl.BlockSpec(memory_space=pltpu.HBM)
    return pl.pallas_call(
        update_kernel,
        out_shape=jax.ShapeDtypeStruct((j_dev, vox_dev), f32),
        in_specs=[hbm, hbm, hbm, vmem, vmem, vmem, hbm],
        out_specs=vmem,
        scratch_shapes=[
            pltpu.VMEM((j_dev, vox_dev), f32),
            pltpu.VMEM((block_vox, width), bf16),
            pltpu.VMEM((n_obs, width), bf16),
            pltpu.VMEM((j_dev, n_obs), f32),
            dma((blocks_dev + 3,)),
            pltpu.VMEM((N_GRP, 2 * j_dev, vox_dev // 2), bf16),
            pltpu.VMEM((members, members), f32),
            pltpu.VMEM((j_dev, members), f32),
            pltpu.VMEM((N_VOX, blocks_dev * CAP + ROWS, width), bf16),
            pltpu.VMEM((N_VOX, blocks_dev * CAP + ROWS, width), bf16),
            pltpu.VMEM((N_GRP, 2 * j_dev, blocks_dev * width // 2), bf16),
            pltpu.VMEM((members, blocks_dev * width), bf16),
            pltpu.VMEM((members, N_VOX * ROWS), f32),
            pltpu.VMEM((n_tiles, *PIECE), f32),
            pltpu.VMEM((N_VOX, *PIECE), f32),
            pltpu.VMEM((n_tiles, *PIECE), f32),
            pltpu.VMEM((QUAD, n_gram // 2, *PIECE), f32),
            pltpu.VMEM((NZ, *TILE), f32),
            pltpu.VMEM((NC, *TILE), f32),
            dma, dma, dma, dma((N_VOX,)), dma, dma, dma((NZ,)), dma((NZ,)), dma((NZ,)), dma((NZ,)),
            dma, dma, dma, dma,
            dma((3,)), dma((3,)), dma((NZ,)), dma((NZ,)), dma, dma,
            dma((2, NZ // 2)), dma((2, NZ // 2)), dma((NZ,)), dma((NZ,)),
        ],
        compiler_params=pltpu.CompilerParams(
            collective_id=0, has_side_effects=True, vmem_limit_bytes=62 << 20
        ),
        name="update",
    )(log_modulus, basis, sensitivity, blocks, observed, noise, perturbation)


def product(a, b):
    return lax.dot_general(
        a, b, (((1,), (0,)), ((), ())), precision=HIGHEST, preferred_element_type=jnp.float32
    )


def inverse(d, k):
    n = d.shape[0]
    lane = lax.broadcasted_iota(jnp.int32, (1, n), 1)
    sub = lax.broadcasted_iota(jnp.int32, (n, 1), 0)
    for p in range(0, n, k):
        cols = [jnp.broadcast_to(d[:, p + j : p + j + 1], (n, n)) for j in range(k)]
        s = [[cols[j][p + i : p + i + 1] for j in range(k)] for i in range(k)]
        inside = (lane >= p) & (lane < p + k)
        rows = [
            jnp.where(inside, (lane == p + i).astype(jnp.float32), d[p + i : p + i + 1])
            for i in range(k)
        ]
        for i in range(k):
            inv = 1.0 / s[i][i]
            rows[i] = rows[i] * inv
            for j in range(i + 1, k):
                s[i][j] = s[i][j] * inv
            for r in range(k):
                if r != i:
                    rows[r] = rows[r] - s[r][i] * rows[i]
                    for j in range(i + 1, k):
                        s[r][j] = s[r][j] - s[r][i] * s[i][j]
        row_in = (sub >= p) & (sub < p + k)
        d = jnp.where(inside | row_in, 0.0, d)
        for j in range(k):
            d = d - jnp.where(row_in, jnp.where(sub == p + j, -1.0, 0.0), cols[j]) * rows[j]
    return d


def solve(gram_ref, cross_ref, damp, between):
    b = SIDE
    eye = lax.broadcasted_iota(jnp.int32, (b, b), 0) == lax.broadcasted_iota(jnp.int32, (b, b), 1)

    def block(i, j):
        found = gram_ref[i * b : (i + 1) * b, j * b : (j + 1) * b]
        return found + jnp.where(eye, damp, 0.0) if i == j else found

    c0, c1, c2 = (cross_ref[:, i * b : (i + 1) * b] for i in range(3))
    a01, a12, a20 = block(0, 1), block(1, 2), block(2, 0)
    a10, a02 = a01.T, a20.T
    i0 = inverse(block(0, 0), PIVOTS)
    u01 = product(i0, a01)
    u02 = product(i0, a02)
    y0 = product(c0, i0)
    i1 = inverse(block(1, 1) - product(a10, u01), PIVOTS)
    a12 = a12 - product(a10, u02)
    a21 = a12.T
    a22 = block(2, 2) - product(a20, u02)
    z1 = c1 - product(y0, a01)
    z2 = c2 - product(y0, a02)
    u12 = product(i1, a12)
    y1 = product(z1, i1)
    between(NZ // 2)
    i2 = inverse(a22 - product(a21, u12), PIVOTS)
    z2 = z2 - product(y1, a12)
    x2 = product(z2, i2)
    x1 = product(z1 - product(x2, a21), i1)
    x0 = product(c0 - product(x1, a10) - product(x2, a20), i0)
    return jnp.concatenate([x0, x1, x2], axis=1)


def on_device(log_modulus, basis, sensitivity, obs_block, observed, noise_scale, perturbation):
    n_obs = sensitivity.shape[0]
    return log_modulus + update(
        log_modulus, basis, sensitivity, obs_block.reshape(1, n_obs),
        observed.reshape(1, n_obs), noise_scale.reshape(1, n_obs), perturbation,
    )


def solution(mesh):
    in_specs = (
        P("grp", "vox"), P(), P("vox", None), P("vox", None), P("vox"), P("vox"), P("grp", "vox"),
    )
    return jax.shard_map(
        on_device, mesh=mesh, in_specs=in_specs, out_specs=P("grp", "vox"), check_vma=False
    )
```

```python
import functools
import math

import jax
import jax.numpy as jnp
from jax import lax
from jax.experimental import pallas as pl
from jax.experimental.pallas import tpu as pltpu
from jax.sharding import PartitionSpec as P

MESH = pl.DeviceIdType.MESH
HIGHEST = lax.Precision.HIGHEST
NX, NY, NZ, NC = 4, 8, 8, 2
N_VOX, N_GRP = NX * NY, NZ * NC
SIDE = 128
PIVOTS = 8
TILE = (8, 128)
PIECE = (16, 128)
QUAD = 4
CAP = 8
ROWS = 16


def remote(src, dst, send_sem, recv_sem, device):
    return pltpu.make_async_remote_copy(
        src_ref=src, dst_ref=dst, send_sem=send_sem, recv_sem=recv_sem,
        device_id=device, device_id_type=MESH,
    )


def update_kernel(
    lm_hbm, basis_hbm, sens_hbm, blk_ref, obs_ref, noise_ref, pert_hbm,
    out_ref,
    lm_ref, basis_ref, sens_ref, pert_ref, in_sem, abuf, gram_ref, cross_ref,
    xout, xin, pbuf, phi, pred_ref, part, rbuf, tot, gbuf, mbuf, msum,
    xs_sem, xr_sem, hs_sem, hr_sem, cs_sem, cr_sem, ds_sem, dr_sem, dps_sem, dpr_sem,
    rs_sem, rr_sem, as_sem, ar_sem, gs_sem, gr_sem, ms_sem, mr_sem, mps_sem, mpr_sem,
    fs_sem, fr_sem, fps_sem, fpr_sem,
):
    g = lax.axis_index("grp")
    v = lax.axis_index("vox")
    z, core = g // NC, g % NC
    x, y = v // NY, v % NY
    partner = z * NC + (1 - core)
    j_dev, vox_dev = lm_ref.shape
    block_vox, width = basis_ref.shape
    blocks_dev = vox_dev // block_vox
    n_obs = sens_ref.shape[0]
    members = j_dev * N_GRP
    scale_root = math.sqrt(members - 1)

    in_blocks = [slice(b * block_vox, (b + 1) * block_vox) for b in range(blocks_dev)]
    pairs = [(lm_hbm.at[:, cut], lm_ref.at[:, cut]) for cut in in_blocks]
    pairs += [(basis_hbm, basis_ref), (sens_hbm, sens_ref), (pert_hbm, pert_ref)]
    fetches = [pltpu.make_async_copy(src, dst, in_sem.at[i]) for i, (src, dst) in enumerate(pairs)]
    for fetch in fetches:
        fetch.start()
    barrier = pltpu.get_barrier_semaphore()

    def greet_vox(i, _):
        pl.semaphore_signal(barrier, inc=1, device_id={"vox": (v + i) % N_VOX}, device_id_type=MESH)
        return 0

    def z_peer(i):
        return ((z + i) % NZ) * NC + core

    def greet_grp(i, _):
        pl.semaphore_signal(barrier, inc=1, device_id={"grp": z_peer(i)}, device_id_type=MESH)
        return 0

    lax.fori_loop(1, N_VOX, greet_vox, 0)
    lax.fori_loop(1, NZ, greet_grp, 0)
    pl.semaphore_signal(barrier, inc=1, device_id={"grp": partner}, device_id_type=MESH)

    strips = []
    for b in range(blocks_dev):
        fetches[b].wait()
        strips.append(jnp.exp(-lm_ref[:, in_blocks[b]]))
    stacked = jnp.concatenate(strips, axis=0).astype(jnp.bfloat16)
    fetches[blocks_dev].wait()
    features = jnp.dot(stacked, basis_ref[...], preferred_element_type=jnp.float32)
    wide = jnp.concatenate([features[b * j_dev : (b + 1) * j_dev] for b in range(blocks_dev)], axis=1)
    f_half = blocks_dev * width // 2
    pbuf[g] = jnp.concatenate([wide[:, :f_half], wide[:, f_half:]], axis=0).astype(jnp.bfloat16)
    lane_half = vox_dev // 2
    pl.semaphore_wait(barrier, N_VOX - 1 + NZ - 1 + 1)

    def peer_copy(i, arriving):
        slot = pbuf.at[((z + NZ - i) % NZ) * NC + core if arriving else g]
        return remote(slot, slot, ds_sem.at[i], dr_sem.at[i], {"grp": z_peer(i)})

    def partner_copy(i, arriving):
        slot = pbuf.at[((z + NZ - i) % NZ) * NC + (1 - core if arriving else core)]
        return remote(slot, slot, dps_sem.at[i], dpr_sem.at[i], {"grp": partner})

    def send_peer(i, _):
        peer_copy(i, False).start()
        return 0

    def forward(i, _):
        peer_copy(i, True).wait_recv()
        partner_copy(i, False).start()
        return 0

    def from_partner(i, _):
        partner_copy(i, True).wait_recv()
        return 0

    lax.fori_loop(1, NZ, send_peer, 0)
    partner_copy(0, False).start()

    z_last = NZ // 2

    def field_part(slot, way, step):
        if step < z_last:
            return abuf.at[slot]
        return abuf.at[slot, :, pl.ds(way * (lane_half // 2), lane_half // 2)]

    def field_copy(way, step, arriving):
        turn = 1 if way == 0 else NZ - 1
        back = step if arriving else step - 1
        slot = ((z + (NZ - turn) * back) % NZ) * NC + core
        ref = field_part(slot, way, step)
        return remote(ref, ref, fs_sem.at[way, step - 1], fr_sem.at[way, step - 1],
                      {"grp": ((z + turn) % NZ) * NC + core})

    def field_partner(i, arriving):
        slot = ((z + NZ - i) % NZ) * NC + (1 - core if arriving else core)
        return remote(abuf.at[slot], abuf.at[slot], fps_sem.at[i], fpr_sem.at[i], {"grp": partner})

    def field_step(step):
        for way in range(2):
            if step > 0:
                field_copy(way, step, True).wait_recv()
            if step < z_last:
                field_copy(way, step + 1, False).start()
        if step in (0, z_last):
            field_partner(step, False).start()
        else:
            field_partner(step, False).start()
            field_partner(NZ - step, False).start()

    lm = lm_ref[...]
    abuf[g] = jnp.concatenate([lm[:, :lane_half], lm[:, lane_half:]], axis=0).astype(jnp.bfloat16)
    field_step(0)

    n_blocks = blocks_dev * N_VOX
    slots = blocks_dev * CAP
    groups = slots // ROWS
    blk = blk_ref[...]
    hit = (lax.broadcasted_iota(jnp.int32, (n_blocks, n_obs), 0) == blk).astype(jnp.float32)
    before = (
        lax.broadcasted_iota(jnp.int32, (n_obs, n_obs), 0)
        < lax.broadcasted_iota(jnp.int32, (n_obs, n_obs), 1)
    ).astype(jnp.float32)
    counts = jnp.dot(
        hit.astype(jnp.bfloat16), before.astype(jnp.bfloat16), preferred_element_type=jnp.float32
    )
    rank = jnp.sum(hit * counts, axis=0, keepdims=True)
    slot_of = blk * CAP + rank.astype(jnp.int32)

    def three(value):
        first = value.astype(jnp.bfloat16).astype(jnp.float32)
        second = (value - first).astype(jnp.bfloat16).astype(jnp.float32)
        return first, second, value - first - second

    observed = obs_ref[...]
    sub = lax.broadcasted_iota(jnp.int32, (8, n_obs), 0)
    tail = jnp.zeros((8, n_obs), jnp.float32)
    for i, term in enumerate((*three(observed), *three(1.0 / noise_ref[...]))):
        tail = jnp.where(sub == i, term, tail)
    fetches[blocks_dev + 1].wait()
    fetches[blocks_dev + 2].wait()
    with_obs = jnp.concatenate([pert_ref[...], tail], axis=0).astype(jnp.bfloat16)
    row_id = lax.broadcasted_iota(jnp.int32, (N_VOX * ROWS, n_obs), 0)
    code = row_id + (slots - ROWS) * lax.shift_right_logical(row_id, ROWS.bit_length() - 1)
    extras = []
    for q in range(groups):
        take = (code == slot_of - ROWS * q).astype(jnp.float32).astype(jnp.bfloat16)
        rows_q = jnp.dot(take, sens_ref[...], preferred_element_type=jnp.float32)
        xout[:, ROWS * q : ROWS * (q + 1), :] = rows_q.astype(jnp.bfloat16).reshape(N_VOX, ROWS, width)
        extras.append(
            lax.dot_general(take, with_obs, (((1,), (1,)), ((), ())), preferred_element_type=jnp.float32)
        )
    beside = jnp.concatenate(extras, axis=1).astype(jnp.bfloat16)
    xout[:, slots : slots + ROWS, :] = beside.reshape(N_VOX, ROWS, width)

    part_rows = slots // NC
    own_half = pl.ds(pl.multiple_of(core * part_rows, 16), part_rows)
    other_half = pl.ds(pl.multiple_of((1 - core) * part_rows, 16), part_rows)
    beside_rows = pl.ds(slots, ROWS)

    def half_copy(i):
        to = (v + i) % N_VOX
        return remote(xout.at[to, own_half], xin.at[v, own_half], hs_sem, hr_sem.at[i], {"vox": to})

    def half_from(i, which):
        slot = xin.at[(v + N_VOX - i) % N_VOX, which]
        return remote(slot, slot, cs_sem, cr_sem, {"grp": partner})

    def send_rows(i, _):
        to = (v + i) % N_VOX
        half_copy(i).start()
        remote(xout.at[to, beside_rows], xin.at[v, beside_rows], xs_sem, xr_sem, {"vox": to}).start()
        return 0

    def pass_half(i, _):
        slot = xin.at[(v + N_VOX - i) % N_VOX, own_half]
        remote(slot, slot, hs_sem, hr_sem.at[i], {"grp": partner}).wait_recv()
        half_from(i, own_half).start()
        return 0

    lax.fori_loop(1, N_VOX, send_rows, 0)
    xin[v] = xout[v]
    lax.fori_loop(1, NZ, forward, 0)
    lax.fori_loop(0, NZ, from_partner, 0)

    def features_of(group):
        d = pbuf[group].astype(jnp.float32)
        return jnp.concatenate([d[:j_dev], d[j_dev:]], axis=1)

    def place_pair(n, _):
        both = jnp.concatenate([features_of(2 * n), features_of(2 * n + 1)], axis=0)
        rows = 2 * j_dev
        phi[pl.ds(pl.multiple_of(n * rows, 16), rows), :] = both.astype(jnp.bfloat16)
        return 0

    lax.fori_loop(0, NZ, place_pair, 0)
    lax.fori_loop(1, N_VOX, pass_half, 0)
    field_step(1)
    got_beside = xin.at[pl.ds(0, N_VOX - 1), beside_rows]
    got_halves = xin.at[pl.ds(0, N_VOX - 1), pl.ds(0, part_rows)]
    pltpu.make_async_copy(got_beside, got_beside, xr_sem).wait()
    pltpu.make_async_copy(got_halves, got_halves, cr_sem).wait()

    n_here = N_VOX * ROWS
    extra = xin[:, slots : slots + ROWS, :].astype(jnp.float32).reshape(n_here, width).T
    per = width // groups
    low = (lax.broadcasted_iota(jnp.int32, (n_here, width), 0) & (ROWS - 1)) < CAP
    u = z % 2 * NC + core
    share = SIDE // QUAD
    n_side = members // SIDE
    sums = jnp.zeros((n_side * share + j_dev, members), jnp.float32)
    lanes = jnp.zeros(TILE, jnp.float32)
    pair = 2 * width
    contract = (((1,), (1,)), ((), ()))
    for q in range(groups):
        rows_q = xin[:, ROWS * q : ROWS * (q + 1), :].astype(jnp.float32).reshape(n_here, width)
        both = jnp.concatenate([jnp.where(low, rows_q, 0.0), jnp.where(low, 0.0, rows_q)], axis=1)
        pred = lax.dot_general(
            phi[:, pair * q : pair * (q + 1)], both.astype(jnp.bfloat16), contract,
            preferred_element_type=jnp.float32,
        )
        pred_ref[...] = pred
        centre = jnp.sum(pred, axis=0, keepdims=True) * (1.0 / members)
        at = per * q + j_dev
        seen = extra[at : at + 1] + extra[at + 1 : at + 2] + extra[at + 2 : at + 3]
        inv_noise = extra[at + 3 : at + 4] + extra[at + 4 : at + 5] + extra[at + 5 : at + 6]
        scale = inv_noise * (1.0 / scale_root)
        scaled = ((pred - centre) * scale).astype(jnp.bfloat16)
        own_pred = pred_ref[pl.ds(pl.multiple_of(g * j_dev, 8), j_dev), :]
        misfit = (seen - own_pred) * inv_noise + extra[per * q : per * q + j_dev]
        misfit = misfit.astype(jnp.bfloat16).astype(jnp.float32)
        some = [
            pred_ref[pl.ds(pl.multiple_of(side * SIDE + u * share, 8), share), :] for side in range(n_side)
        ]
        left = jnp.concatenate([(p - centre) * scale for p in some] + [misfit], axis=0)
        left = left.astype(jnp.bfloat16)
        sums = sums + lax.dot_general(left, scaled, contract, preferred_element_type=jnp.float32)
        squares = misfit * misfit
        for i in range(j_dev // 8):
            for c in range(n_here // 128):
                lanes = lanes + squares[8 * i : 8 * i + 8, 128 * c : 128 * c + 128]

    n_row, n_col = j_dev // 8, members // 128
    strips_u = share // 8
    gram_at = [(side, strip, (side + turn) % n_side)
               for side in range(n_side) for strip in range(strips_u) for turn in range(2)]
    tiles = [sums[side * share + 8 * strip : side * share + 8 * strip + 8, SIDE * k : SIDE * (k + 1)]
             for side, strip, k in gram_at]
    n_gram = len(tiles)
    n_pieces = n_gram // 2
    tiles.append(lanes)
    first_cross = n_side * share
    for i in range(n_row):
        for c in range(n_col):
            tiles.append(sums[first_cross + 8 * i : first_cross + 8 * i + 8, 128 * c : 128 * c + 128])
    for t, tile in enumerate(tiles):
        part[t // 2, t % 2 * 8 : t % 2 * 8 + 8] = tile
    n_tiles = len(tiles) // 2

    def send_part(i, _):
        t = (v + i) % n_tiles

        @pl.when(t != v)
        def _():
            remote(part.at[t], rbuf.at[v], rs_sem, rr_sem, {"vox": t}).start()

        return 0

    lax.fori_loop(0, n_tiles, send_part, 0)

    @pl.when(v < n_tiles)
    def _():
        rbuf[v] = part[v]
        got = rbuf.at[pl.ds(0, N_VOX - 1)]
        pltpu.make_async_copy(got, got, rr_sem).wait()
        tot[v] = jnp.sum(rbuf[...], axis=0)

        def spread(i, _):
            remote(tot.at[v], tot.at[v], as_sem, ar_sem, {"vox": (v + i) % N_VOX}).start()
            return 0

        lax.fori_loop(1, N_VOX, spread, 0)

    field_step(2)

    @pl.when(v < n_tiles)
    def _():
        most = tot.at[pl.ds(0, n_tiles - 1)]
        pltpu.make_async_copy(most, most, ar_sem).wait()

    @pl.when(v >= n_tiles)
    def _():
        whole = tot.at[pl.ds(0, n_tiles)]
        pltpu.make_async_copy(whole, whole, ar_sem).wait()

    gbuf[u] = tot[0:n_pieces]
    mbuf[z] = tot[n_pieces, 0:8]
    beyond = {"grp": (z + 1 - z % 2 * 2) * NC + core}
    u_beyond = (1 - z % 2) * NC + core

    def gram_copy(n, slot, to):
        return remote(gbuf.at[slot], gbuf.at[slot], gs_sem.at[n], gr_sem.at[n], to)

    def squares_copy(i, arriving):
        slot = mbuf.at[(z + NZ - i) % NZ if arriving else z]
        return remote(slot, slot, ms_sem.at[i], mr_sem.at[i], {"grp": z_peer(i)})

    gram_copy(0, u, beyond).start()
    gram_copy(1, u, {"grp": partner}).start()

    def squares_send(i, _):
        squares_copy(i, False).start()
        return 0

    lax.fori_loop(1, NZ, squares_send, 0)
    for i in range(n_row):
        for c in range(n_col):
            t = n_gram + 1 + i * n_col + c
            cross_ref[8 * i : 8 * i + 8, 128 * c : 128 * c + 128] = tot[t // 2, t % 2 * 8 : t % 2 * 8 + 8]
    gram_copy(0, u_beyond, beyond).wait_recv()
    gram_copy(2, u_beyond, {"grp": partner}).start()

    def squares_wait(i, _):
        squares_copy(i, True).wait_recv()
        return 0

    lax.fori_loop(1, NZ, squares_wait, 0)
    msum[core] = jnp.sum(mbuf[...], axis=0)
    squares_across = remote(msum.at[core], msum.at[core], mps_sem, mpr_sem, {"grp": partner})
    squares_across.start()
    gram_copy(1, z % 2 * NC + 1 - core, {"grp": partner}).wait_recv()
    gram_copy(2, (1 - z % 2) * NC + 1 - core, {"grp": partner}).wait_recv()
    for n in range(QUAD):
        for t, (side, strip, k) in enumerate(gram_at):
            row = side * SIDE + n * share + 8 * strip
            gram_ref[row : row + 8, SIDE * k : SIDE * (k + 1)] = gbuf[n, t // 2, t % 2 * 8 : t % 2 * 8 + 8]
    remote(msum.at[1 - core], msum.at[1 - core], mps_sem, mpr_sem, {"grp": partner}).wait_recv()
    damping = jnp.sum(msum[0] + msum[1], keepdims=True) * (1.0 / (members * n_obs * N_VOX))
    field_step(3)
    weights = solve(gram_ref, cross_ref, damping, field_step).astype(jnp.bfloat16)

    def field_from(i, _):
        field_partner(i, True).wait_recv()
        return 0

    lax.fori_loop(0, NZ, field_from, 0)
    col = lax.broadcasted_iota(jnp.int32, (members, 2 * members), 1)
    row = lax.broadcasted_iota(jnp.int32, (members, 2 * members), 0)
    group = jnp.floor((row.astype(jnp.float32) + 0.5) * (1.0 / j_dev)).astype(jnp.int32)
    place_of = row + group * j_dev
    spread_weights = jnp.concatenate(
        [
            jnp.dot(weights, (col == place_of + j_dev * h).astype(jnp.bfloat16),
                    preferred_element_type=jnp.float32)
            for h in range(2)
        ],
        axis=0,
    ).astype(jnp.bfloat16)
    piece = 512
    for n in range(lane_half // piece):
        cut = slice(n * piece, (n + 1) * piece)
        field = abuf[:, :, cut].reshape(2 * members, piece)
        mixture = jnp.dot(spread_weights, field, preferred_element_type=jnp.float32) * (1.0 / scale_root)
        for h in range(2):
            cols = slice(h * lane_half + n * piece, h * lane_half + (n + 1) * piece)
            out_ref[:, cols] = mixture[h * j_dev : (h + 1) * j_dev]

    pltpu.make_async_copy(got_beside, got_beside, xs_sem).wait()
    pltpu.make_async_copy(got_halves, got_halves, hs_sem).wait()
    pltpu.make_async_copy(got_halves, got_halves, cs_sem).wait()
    def grp_sent(i, _):
        peer_copy(i, False).wait_send()
        squares_copy(i, False).wait_send()
        return 0

    def partner_sent(i, _):
        for copy in (partner_copy(i, False), field_partner(i, False)):
            copy.wait_send()
        return 0

    lax.fori_loop(1, NZ, grp_sent, 0)
    lax.fori_loop(0, NZ, partner_sent, 0)
    for n in range(3):
        gram_copy(n, u, {"grp": partner}).wait_send()
    squares_across.wait_send()
    for way in range(2):
        for step in range(1, z_last + 1):
            field_copy(way, step, False).wait_send()

    @pl.when(v < n_tiles)
    def _():
        sent = part.at[pl.ds(0, n_tiles - 1)]
        pltpu.make_async_copy(sent, sent, rs_sem).wait()
        spread_all = rbuf.at[pl.ds(0, N_VOX - 1)]
        pltpu.make_async_copy(spread_all, spread_all, as_sem).wait()

    @pl.when(v >= n_tiles)
    def _():
        sent = part.at[pl.ds(0, n_tiles)]
        pltpu.make_async_copy(sent, sent, rs_sem).wait()


def update(log_modulus, basis, sensitivity, blocks, observed, noise, perturbation):
    j_dev, vox_dev = log_modulus.shape
    block_vox, width = basis.shape
    blocks_dev = vox_dev // block_vox
    n_obs = sensitivity.shape[0]
    members = j_dev * N_GRP
    n_gram = (members // SIDE) * (SIDE // QUAD // 8) * 2
    n_tiles = (n_gram + 1 + (j_dev // 8) * (members // 128)) // 2
    f32, bf16 = jnp.float32, jnp.bfloat16
    dma = pltpu.SemaphoreType.DMA
    vmem = pl.BlockSpec(memory_space=pltpu.VMEM)
    hbm = pl.BlockSpec(memory_space=pltpu.HBM)
    return pl.pallas_call(
        update_kernel,
        out_shape=jax.ShapeDtypeStruct((j_dev, vox_dev), f32),
        in_specs=[hbm, hbm, hbm, vmem, vmem, vmem, hbm],
        out_specs=vmem,
        scratch_shapes=[
            pltpu.VMEM((j_dev, vox_dev), f32),
            pltpu.VMEM((block_vox, width), bf16),
            pltpu.VMEM((n_obs, width), bf16),
            pltpu.VMEM((j_dev, n_obs), f32),
            dma((blocks_dev + 3,)),
            pltpu.VMEM((N_GRP, 2 * j_dev, vox_dev // 2), bf16),
            pltpu.VMEM((members, members), f32),
            pltpu.VMEM((j_dev, members), f32),
            pltpu.VMEM((N_VOX, blocks_dev * CAP + ROWS, width), bf16),
            pltpu.VMEM((N_VOX, blocks_dev * CAP + ROWS, width), bf16),
            pltpu.VMEM((N_GRP, 2 * j_dev, blocks_dev * width // 2), bf16),
            pltpu.VMEM((members, blocks_dev * width), bf16),
            pltpu.VMEM((members, N_VOX * ROWS), f32),
            pltpu.VMEM((n_tiles, *PIECE), f32),
            pltpu.VMEM((N_VOX, *PIECE), f32),
            pltpu.VMEM((n_tiles, *PIECE), f32),
            pltpu.VMEM((QUAD, n_gram // 2, *PIECE), f32),
            pltpu.VMEM((NZ, *TILE), f32),
            pltpu.VMEM((NC, *TILE), f32),
            dma, dma, dma, dma((N_VOX,)), dma, dma, dma((NZ,)), dma((NZ,)), dma((NZ,)), dma((NZ,)),
            dma, dma, dma, dma,
            dma((3,)), dma((3,)), dma((NZ,)), dma((NZ,)), dma, dma,
            dma((2, NZ // 2)), dma((2, NZ // 2)), dma((NZ,)), dma((NZ,)),
        ],
        compiler_params=pltpu.CompilerParams(
            collective_id=0, has_side_effects=True, vmem_limit_bytes=62 << 20
        ),
        name="update",
    )(log_modulus, basis, sensitivity, blocks, observed, noise, perturbation)


def product(a, b):
    return lax.dot_general(
        a, b, (((1,), (0,)), ((), ())), precision=HIGHEST, preferred_element_type=jnp.float32
    )


def inverse(d, k):
    n = d.shape[0]
    lane = lax.broadcasted_iota(jnp.int32, (1, n), 1)
    sub = lax.broadcasted_iota(jnp.int32, (n, 1), 0)
    for p in range(0, n, k):
        cols = [jnp.broadcast_to(d[:, p + j : p + j + 1], (n, n)) for j in range(k)]
        s = [[cols[j][p + i : p + i + 1] for j in range(k)] for i in range(k)]
        inside = (lane >= p) & (lane < p + k)
        rows = [
            jnp.where(inside, (lane == p + i).astype(jnp.float32), d[p + i : p + i + 1])
            for i in range(k)
        ]
        for i in range(k):
            inv = 1.0 / s[i][i]
            rows[i] = rows[i] * inv
            for j in range(i + 1, k):
                s[i][j] = s[i][j] * inv
            for r in range(k):
                if r != i:
                    rows[r] = rows[r] - s[r][i] * rows[i]
                    for j in range(i + 1, k):
                        s[r][j] = s[r][j] - s[r][i] * s[i][j]
        row_in = (sub >= p) & (sub < p + k)
        d = jnp.where(inside | row_in, 0.0, d)
        for j in range(k):
            d = d - jnp.where(row_in, jnp.where(sub == p + j, -1.0, 0.0), cols[j]) * rows[j]
    return d


def solve(gram_ref, cross_ref, damp, between):
    b = SIDE
    eye = lax.broadcasted_iota(jnp.int32, (b, b), 0) == lax.broadcasted_iota(jnp.int32, (b, b), 1)

    def block(i, j):
        found = gram_ref[i * b : (i + 1) * b, j * b : (j + 1) * b]
        return found + jnp.where(eye, damp, 0.0) if i == j else found

    c0, c1, c2 = (cross_ref[:, i * b : (i + 1) * b] for i in range(3))
    a01, a12, a20 = block(0, 1), block(1, 2), block(2, 0)
    a10, a02 = a01.T, a20.T
    i0 = inverse(block(0, 0), PIVOTS)
    u01 = product(i0, a01)
    u02 = product(i0, a02)
    y0 = product(c0, i0)
    i1 = inverse(block(1, 1) - product(a10, u01), PIVOTS)
    a12 = a12 - product(a10, u02)
    a21 = a12.T
    a22 = block(2, 2) - product(a20, u02)
    z1 = c1 - product(y0, a01)
    z2 = c2 - product(y0, a02)
    u12 = product(i1, a12)
    y1 = product(z1, i1)
    between(NZ // 2)
    i2 = inverse(a22 - product(a21, u12), PIVOTS)
    z2 = z2 - product(y1, a12)
    x2 = product(z2, i2)
    x1 = product(z1 - product(x2, a21), i1)
    x0 = product(c0 - product(x1, a10) - product(x2, a20), i0)
    return jnp.concatenate([x0, x1, x2], axis=1)


def on_device(log_modulus, basis, sensitivity, obs_block, observed, noise_scale, perturbation):
    n_obs = sensitivity.shape[0]
    return log_modulus + update(
        log_modulus, basis, sensitivity, obs_block.reshape(1, n_obs),
        observed.reshape(1, n_obs), noise_scale.reshape(1, n_obs), perturbation,
    )


def solution(mesh):
    in_specs = (
        P("grp", "vox"), P(), P("vox", None), P("vox", None), P("vox"), P("vox"), P("grp", "vox"),
    )
    return jax.shard_map(
        on_device, mesh=mesh, in_specs=in_specs, out_specs=P("grp", "vox"), check_vma=False
    )
```
